256 devices in a mesh: prow: 8 (over z_hi, x), pcol: 32 (over y, z_lo, core).
Axes of the slice: x: 4, y: 4, z: 8 (z_hi: 2, z_lo: 4; z = z_hi * 4 + z_lo), core: 2. Of those that a mesh axis runs over, the one named last changes fastest.
Arguments:
- ancestor_inverse: bfloat16 [12288, 12288], P('prow', 'pcol'), may hold values from -0.0546875 to 0.0546875
- factor_panel: bfloat16 [12288, 4096], P('prow', 'pcol'), may hold values from -0.67578125 to 0.67578125
- pivot_inverse: float32 [512, 4096], P('prow', 'pcol'), may hold values from -6 to 6
- sn_size: int32 [8], replicated, may hold values from 128 to 512, as said below
- anc_list: int32 [8, 48], replicated, may hold values from 0 to 95, all different within a row
Outputs:
- ainv_cols: bfloat16 [4096, 12288], P('pcol', 'prow')
- diag_inverse: float32 [512, 4096], P('prow', 'pcol')
The draws below stay inside these ranges and needn't reach their ends.
Inputs may be any that keep to these rules, and one draw needn't show every extreme that they name: `sn_size`: every supernode has between 128 and 512 live columns; some supernode has exactly 512 and some exactly 128. `anc_list`: each row lists 48 distinct ancestor blocks; every block is listed by some supernode.
All inputs are finite; a program needn't handle non-finite values.
Results may differ from the reference program's by a relative error of at most 0.0018.
Values may be sent and summed in bfloat16 or wider, within the bound.
A program may use at most 128 MiB of HBM per device.

```python
import jax
import jax.numpy as jnp
from jax import lax

AB = 128
W = 512
SN = 8
A = 12288
NA = 96
NR = 48
K = 4096


def draw_sn_size(key, part):
    key = jax.random.fold_in(key, 11)
    first, second, third = jax.random.split(key, 3)
    sizes = jax.random.randint(first, (SN,), W // 4, W + 1).astype(jnp.int32)
    big_at = jax.random.randint(second, (), 0, SN)
    small_at = (big_at + 1 + jax.random.randint(third, (), 0, SN - 1)) % SN
    sizes = sizes.at[big_at].set(W)
    sizes = sizes.at[small_at].set(W // 4)
    return sizes.astype(jnp.int32)


def steps_of(stream_key, dims, cuts, smallest, high):
    level, own = 1.0, jax.random.fold_in(stream_key, 6)
    for dim, parts in cuts:
        steps = jnp.exp(jax.random.uniform(jax.random.fold_in(own, dim), (parts,), jnp.float32, smallest / len(cuts), high / len(cuts)))
        level = level * jnp.repeat(steps, dims[dim] // parts).reshape([-1 if axis == dim else 1 for axis in range(len(dims))])
    return level


def picks_of(rng, rows, count, top, lift):
    ranking = jax.random.permutation(jax.random.fold_in(rng, 1), count)
    pull = ranking
    for power in range(3):
        pull = pull * pull // count
    pull = pull * lift // count
    chance = jax.random.randint(jax.random.fold_in(rng, 2), (rows, count), 0, 4096) + pull
    sure = jax.random.permutation(jax.random.fold_in(rng, 3), rows)[jnp.arange(count) % rows]
    chance = jnp.where(jnp.arange(rows)[:, None] == sure[None, :], 1 << 14, chance)
    priority = chance * count + jnp.arange(count)
    return lax.top_k(priority.astype(jnp.int32), top)[1].astype(jnp.int32)


def normal_values(stream_key, extent, width, limit, shards=(), kind=jnp.bfloat16):
    entries = jax.random.normal(stream_key, extent, jnp.float32) * width
    if len(shards) > 0:
        entries = steps_of(stream_key, extent, shards, -0.22, 0.18) * entries
    return jnp.clip(entries, min=-limit, max=limit).astype(kind)


def setup_inputs(seed: int = 0) -> dict:
    arg_keys = jax.random.split(jax.random.key(seed), 6)
    ancestor_inverse = normal_values(arg_keys[0], (A, A), A ** -0.5, 0.0546875, ((0, 8), (1, 32)))
    factor_panel = normal_values(arg_keys[1], (A, K), ((2.0 / A) ** 0.25), 0.67578125, ((0, 8), (1, 32)))
    pivot_inverse = normal_values(arg_keys[2], (W, K), 1.0, 6.0, ((0, 8), (1, 32)), jnp.float32)
    sn_size = draw_sn_size(jax.random.fold_in(arg_keys[5], 71), 0)
    anc_list = picks_of(arg_keys[4], SN, NA, NR, 8192)
    return {"ancestor_inverse": ancestor_inverse, "factor_panel": factor_panel, "pivot_inverse": pivot_inverse, "sn_size": sn_size, "anc_list": anc_list}


def live_mask(sn_size, anc_list):
    blocks = jnp.arange(NA, dtype=jnp.int32)
    block_live = jnp.any(anc_list[:, :, None] == blocks[None, None, :], axis=1).astype(jnp.float32)
    rows = jnp.arange(A, dtype=jnp.int32) // AB
    row_live = block_live.T[rows]
    cols = jnp.arange(K, dtype=jnp.int32)
    owner = cols // W
    col_live = ((cols % W) < sn_size[owner]).astype(jnp.float32)
    return row_live[:, owner] * col_live[None, :]


def reference(ancestor_inverse, factor_panel, pivot_inverse, sn_size, anc_list):
    live = live_mask(sn_size, anc_list)
    lhat = (factor_panel.astype(jnp.float32) * live).astype(jnp.bfloat16)
    sum_full = jnp.dot(ancestor_inverse, lhat, preferred_element_type=jnp.float32)
    ainv = (-(sum_full * live)).astype(jnp.bfloat16)
    pieces = []
    for k in range(SN):
        lk = lhat[:, k * W:(k + 1) * W]
        yk = ainv[:, k * W:(k + 1) * W]
        pieces.append(lax.dot_general(lk, yk, (((0,), (0,)), ((), ())), preferred_element_type=jnp.float32))
    corr = jnp.concatenate(pieces, axis=1)
    cols = jnp.arange(K, dtype=jnp.int32)
    owner = cols // W
    size_col = sn_size[owner]
    rows_a = jnp.arange(W, dtype=jnp.int32)
    keep = ((rows_a[:, None] < size_col[None, :]) & ((cols % W) < size_col)[None, :]).astype(jnp.float32)
    diag = (pivot_inverse - corr) * keep
    return ainv.T, diag
```

```python
import jax
import jax.numpy as jnp
from jax import lax
from jax.experimental import pallas as pl
from jax.experimental.pallas import tpu as pltpu
from jax.sharding import PartitionSpec as P

AB = 128
W = 512
MESH = pl.DeviceIdType.MESH
MCH = 4


def kernel(
    a_ref, l_ref, piv_ref, sn_ref, anc_ref, out_ref, diag_ref,
    abuf, lhat, lbuf, lead, live, acc, cown, csend, crecv, abf, corr, drecv,
    ld_sem, lz_s, l_r, lx_s, a_s, a_r, ab_r, c_s, c_r, h_s, h_r, d_s, d_r,
):
    rows = l_ref.shape[0]
    mrows = rows // MCH
    half = rows // 2
    kw = a_ref.shape[1]
    tiles = mrows // AB
    p = lax.axis_index("prow")
    q = lax.axis_index("pcol")
    x, zh = p % 4, p // 4
    y, zl, c = q // 8, (q // 2) % 4, q % 2
    z = zh * 4 + zl
    k = q // 4

    def dev(x_, y_, z_, c_):
        return ((z_ // 4) * 4 + x_, y_ * 8 + (z_ % 4) * 2 + c_)

    def at_x(d):
        return dev((x + d) % 4, y, z, c)

    def at_y(d):
        return dev(x, (y + d) % 4, z, c)

    def at_z(z_):
        return dev(x, y, z_, c)

    sib = dev(x, y, z, 1 - c)

    def rcopy(src, dst, ssem, rsem, device):
        return pltpu.make_async_remote_copy(
            src_ref=src, dst_ref=dst, send_sem=ssem, recv_sem=rsem,
            device_id=device, device_id_type=MESH)

    barrier = pltpu.get_barrier_semaphore()
    partners = [at_z((z + d) % 8) for d in range(1, 8)]
    partners += [dev((x + d) % 4, y, ((zh + e) % 2) * 4 + zl, c)
                 for d in range(1, 4) for e in range(2)]
    partners += [at_y(1), at_y(3), sib]
    for partner in partners:
        pl.semaphore_signal(barrier, inc=1, device_id=partner, device_id_type=MESH)

    def mchunk(m):
        return pl.ds(m * mrows, mrows)

    def ablk(y_, c_, r):
        return abuf.at[y_, r, pl.ds(pl.multiple_of(c_ * kw, 128), kw)]

    def load(m):
        r = mchunk(m)
        return pltpu.make_async_copy(a_ref.at[r, :], ablk(y, c, r), ld_sem.at[m])

    for m in range(MCH):
        load(m).start()

    ids = p * (rows // AB) + lax.broadcasted_iota(jnp.int32, (16, anc_ref.shape[1]), 0)
    hit = jnp.where(ids == anc_ref[pl.ds(k, 1), :], 1.0, 0.0)
    row_live = jnp.max(hit, axis=1, keepdims=True)
    cols = (q % 4) * AB + lax.broadcasted_iota(jnp.int32, (1, AB), 1)
    col_live = jnp.where(cols < sn_ref[k], 1.0, 0.0)
    live[...] = row_live * col_live
    for b in range(rows // AB):
        r = pl.ds(b * AB, AB)
        lhat[r, :] = (l_ref[r, :].astype(jnp.float32) * live[b:b + 1, :]).astype(jnp.bfloat16)

    pl.semaphore_wait(barrier, len(partners))

    def lslot(xs, zs):
        lane = ((zs % 4 - zl + 4) % 4) * AB
        return lbuf.at[(zs // 4) * 2 + xs, :, pl.ds(pl.multiple_of(lane, 128), AB)]

    def lsem(xs, zs):
        return l_r.at[xs * 8 + zs]

    zsends = []
    for hh in range(2):
        for e in range(2):
            tz = (x % 2) * 2 + hh
            to = e * 4 + tz
            lane = ((zl - tz + 4) % 4) * AB
            dst = lbuf.at[zh * 2 + x // 2, :, pl.ds(pl.multiple_of(lane, 128), AB)]
            src = lhat.at[pl.ds(hh * half, half), :]
            rem = rcopy(src, dst, lz_s.at[hh * 2 + e], lsem(x // 2, z), at_z(to))
            loc = pltpu.make_async_copy(src, dst, lsem(x // 2, z))
            zsends.append((to != z, rem))

            @pl.when(to != z)
            def _(rem=rem):
                rem.start()

            @pl.when(to == z)
            def _(loc=loc):
                loc.start()

    def a_own(m):
        r = mchunk(m)
        blk = ablk(y, c, r)
        return [rcopy(blk, blk, a_s.at[m, 0], a_r.at[m, 0], at_y(1)),
                rcopy(blk, blk, a_s.at[m, 1], a_r.at[m, 1], at_y(3)),
                rcopy(blk, blk, a_s.at[m, 2], ab_r.at[m, 0], sib)]

    hr = mrows // 2

    def a_fwd(m):
        lo, hi = pl.ds(m * mrows, hr), pl.ds(m * mrows + hr, hr)
        r = mchunk(m)
        ym, yp = (y + 3) % 4, (y + 1) % 4
        return [rcopy(ablk(ym, c, lo), ablk(ym, c, lo), a_s.at[m, 3], a_r.at[m, 2], at_y(1)),
                rcopy(ablk(yp, c, hi), ablk(yp, c, hi), a_s.at[m, 4], a_r.at[m, 3], at_y(3)),
                rcopy(ablk(ym, c, r), ablk(ym, c, r), a_s.at[m, 5], ab_r.at[m, 1], sib),
                rcopy(ablk(yp, c, r), ablk(yp, c, r), a_s.at[m, 6], ab_r.at[m, 2], sib)]

    def a_opp(m):
        lo, hi = pl.ds(m * mrows, hr), pl.ds(m * mrows + hr, hr)
        yo = (y + 2) % 4
        return [rcopy(ablk(yo, c, lo), ablk(yo, c, lo), a_s.at[m, 7], ab_r.at[m, 3], sib),
                rcopy(ablk(yo, c, hi), ablk(yo, c, hi), a_s.at[m, 8], ab_r.at[m, 4], sib)]

    def wait_into(ref, sem):
        pltpu.make_async_copy(ref, ref, sem).wait()

    for m in range(MCH):
        load(m).wait()
        for cp in a_own(m):
            cp.start()

    zmate = z + 1 - 2 * (z % 2)

    def hblk(zb, cb):
        return lead.at[:, pl.ds(pl.multiple_of(((zb % 2) * 2 + cb) * AB, 128), AB)]

    h_own = [rcopy(lhat, hblk(z, c), h_s.at[0], h_r.at[0], at_z(zmate)),
             rcopy(lhat, hblk(z, c), h_s.at[1], h_r.at[1], sib)]
    h_fwd = rcopy(hblk(zmate, c), hblk(zmate, c), h_s.at[2], h_r.at[2], sib)
    h_loc = pltpu.make_async_copy(lhat, hblk(z, c), h_s.at[3])
    h_loc.start()

    is_src = x % 2 == zl // 2
    order = [0, 1, 7, 2, 6, 3, 5, 4]

    def x_src(i):
        zs = (z + order[i]) % 8
        xs = x // 2
        return [rcopy(lslot(xs, zs), lslot(xs, zs), lx_s.at[i * 2 + n], lsem(xs, zs), at_x(d))
                for n, d in enumerate((1, 3))]

    def x_mid(i):
        zs = (z + order[i]) % 8
        xm, xp = ((x + 3) % 4) // 2, ((x + 1) % 4) // 2
        return (zs, xm, xp,
                rcopy(lslot(xm, zs), lslot(xm, zs), lx_s.at[i], lsem(xm, zs), at_x(1)),
                rcopy(lslot(xp, zs), lslot(xp, zs), lx_s.at[i], lsem(xp, zs), at_x(3)))

    for i in range(8):
        @pl.when(is_src)
        def _(i=i):
            zs = (z + order[i]) % 8
            wait_into(lslot(x // 2, zs), lsem(x // 2, zs))
            for cp in x_src(i):
                cp.start()

        @pl.when(jnp.logical_not(is_src))
        def _(i=i):
            zs, xm, xp, up, down = x_mid(i)
            wait_into(lslot(xm, zs), lsem(xm, zs))

            @pl.when(zs % 2 == 0)
            def _():
                up.start()

            wait_into(lslot(xp, zs), lsem(xp, zs))

            @pl.when(zs % 2 == 1)
            def _():
                down.start()

        if i % 2 == 1:
            m = i // 2
            r = mchunk(m)
            cps = a_fwd(m)
            wait_into(ablk((y + 3) % 4, c, r), a_r.at[m, 0])
            cps[0].start()
            cps[2].start()
            wait_into(ablk((y + 1) % 4, c, r), a_r.at[m, 1])
            cps[1].start()
            cps[3].start()
        if i == 5:
            for cp in h_own:
                cp.start()

    for i in range(8):
        @pl.when(is_src)
        def _(i=i):
            zs = (z + order[i]) % 8
            xo = 1 - x // 2
            wait_into(lslot(xo, zs), lsem(xo, zs))

    for m in range(MCH):
        yo = (y + 2) % 4
        cps = a_opp(m)
        wait_into(ablk(yo, c, pl.ds(m * mrows, hr)), a_r.at[m, 2])
        cps[0].start()
        wait_into(ablk(yo, c, pl.ds(m * mrows + hr, hr)), a_r.at[m, 3])
        cps[1].start()

    def c_copy(m, j):
        return rcopy(csend.at[m, j - 1], crecv.at[m, j - 1], c_s.at[m, j - 1], c_r.at[m, j - 1],
                     at_z(zh * 4 + (zl + j) % 4))

    @pl.loop(0, MCH)
    def _(m):
        r = pl.ds(pl.multiple_of(m * mrows, mrows), mrows)
        lo = pl.ds(pl.multiple_of(m * mrows, hr), hr)
        hi = pl.ds(pl.multiple_of(m * mrows + hr, hr), hr)
        oc = 1 - c
        wait_into(ablk(y, oc, r), ab_r.at[m, 0])
        wait_into(ablk((y + 3) % 4, oc, r), ab_r.at[m, 1])
        wait_into(ablk((y + 1) % 4, oc, r), ab_r.at[m, 2])
        wait_into(ablk((y + 2) % 4, oc, lo), ab_r.at[m, 3])
        wait_into(ablk((y + 2) % 4, oc, hi), ab_r.at[m, 4])
        acc[...] = jnp.dot(abuf[0, r, :], lbuf[0], preferred_element_type=jnp.float32)
        for yy in range(1, 4):
            acc[...] += jnp.dot(abuf[yy, r, :], lbuf[yy], preferred_element_type=jnp.float32)
        cown[r, :] = acc[:, 0:AB]
        for j in range(1, 4):
            for t in range(tiles):
                part = acc[t * AB:(t + 1) * AB, j * AB:(j + 1) * AB]
                top = jnp.max(jnp.abs(part), axis=0, keepdims=True)
                e = jnp.clip(jnp.floor(jnp.log2(jnp.maximum(top, 1e-30))) + 1.0, -90.0, 90.0)
                v = jnp.clip(jnp.round(part * jnp.exp2(15.0 - e)), -32767.0, 32767.0)
                csend[m, j - 1, t, 0:AB, :] = v.astype(jnp.int32).astype(jnp.int16)
                csend[m, j - 1, t, AB:AB + 16, :] = jnp.broadcast_to(
                    e.astype(jnp.int32), (16, AB)).astype(jnp.int16)
            c_copy(m, j).start()

    wait_into(hblk(zmate, c), h_r.at[0])
    h_fwd.start()
    h_loc.wait()
    wait_into(hblk(z, 1 - c), h_r.at[1])
    wait_into(hblk(zmate, 1 - c), h_r.at[2])

    corr[...] = jnp.zeros_like(corr)

    @pl.loop(0, MCH)
    def _(m):
        r = pl.ds(pl.multiple_of(m * mrows, mrows), mrows)
        for j in range(1, 4):
            wait_into(crecv.at[m, j - 1], c_r.at[m, j - 1])
        for t in range(tiles):
            at = pl.multiple_of(m * mrows + t * AB, AB)
            s = cown[pl.ds(at, AB), :]
            for j in range(1, 4):
                v = crecv[m, j - 1, t, 0:AB, :].astype(jnp.int32).astype(jnp.float32)
                e = crecv[m, j - 1, t, AB:AB + 16, :].astype(jnp.int32).astype(jnp.float32)
                s = s + v * jnp.exp2(e[0:1, :] - 15.0)
            s = -(s * live[pl.ds(m * tiles + t, 1), :])
            abf[t * AB:(t + 1) * AB, :] = s.astype(jnp.bfloat16)
            out_ref[:, pl.ds(at, AB)] = s.T.astype(jnp.bfloat16)
        corr[...] += lax.dot_general(
            lead[r, :], abf[...], (((0,), (0,)), ((), ())), preferred_element_type=jnp.float32)

    lrows = diag_ref.shape[0]

    def mine(p_):
        return pl.ds(pl.multiple_of(p_ * lrows, lrows), lrows)

    dcopies = []
    for d in range(1, 8):
        to = (p + d) % 8
        cp = rcopy(corr.at[mine(to), :], drecv.at[d - 1], d_s.at[d - 1], d_r.at[d - 1], (to, q))
        cp.start()
        dcopies.append(cp)
    total = corr[mine(p), :]
    for d in range(1, 8):
        wait_into(drecv.at[d - 1], d_r.at[d - 1])
        total = total + drecv[d - 1]
    lead_id = p * lrows + lax.broadcasted_iota(jnp.int32, (lrows, AB), 0)
    keep = jnp.where(lead_id < sn_ref[k], 1.0, 0.0) * col_live
    diag_ref[...] = (piv_ref[...] - total) * keep

    for cond, rem in zsends:
        @pl.when(cond)
        def _(rem=rem):
            rem.wait_send()
    for i in range(8):
        @pl.when(is_src)
        def _(i=i):
            for cp in x_src(i):
                cp.wait_send()

        @pl.when(jnp.logical_not(is_src))
        def _(i=i):
            x_mid(i)[3].wait_send()
    for m in range(MCH):
        for cp in a_own(m) + a_fwd(m) + a_opp(m):
            cp.wait_send()
        for j in range(1, 4):
            c_copy(m, j).wait_send()
    for cp in h_own + [h_fwd] + dcopies:
        cp.wait_send()


def per_device(ancestor_inverse, factor_panel, pivot_inverse, sn_size, anc_list):
    rows, cols = factor_panel.shape
    kw = ancestor_inverse.shape[1]
    lrows = pivot_inverse.shape[0]
    mrows = rows // MCH
    tiles = mrows // AB
    vm, dma = pltpu.VMEM, pltpu.SemaphoreType.DMA
    bf, f32 = jnp.bfloat16, jnp.float32
    vspec = pl.BlockSpec(memory_space=pltpu.VMEM)
    return pl.pallas_call(
        kernel,
        out_shape=(jax.ShapeDtypeStruct((cols, rows), bf),
                   jax.ShapeDtypeStruct((lrows, cols), f32)),
        in_specs=[pl.BlockSpec(memory_space=pl.ANY), vspec, vspec,
                  pl.BlockSpec(memory_space=pltpu.SMEM), vspec],
        out_specs=(vspec, vspec),
        scratch_shapes=[
            vm((4, rows, 2 * kw), bf),
            vm((rows, cols), bf),
            vm((4, 2 * kw, 4 * cols), bf),
            vm((rows, W), bf),
            vm((16, cols), f32),
            vm((mrows, 4 * cols), f32),
            vm((rows, cols), f32),
            vm((MCH, 3, tiles, AB + 16, cols), jnp.int16),
            vm((MCH, 3, tiles, AB + 16, cols), jnp.int16),
            vm((mrows, cols), bf),
            vm((W, cols), f32),
            vm((7, lrows, cols), f32),
            dma((MCH,)), dma((4,)), dma((16,)), dma((16,)),
            dma((MCH, 9)), dma((MCH, 4)), dma((MCH, 5)),
            dma((MCH, 3)), dma((MCH, 3)),
            dma((4,)), dma((3,)), dma((7,)), dma((7,)),
        ],
        compiler_params=pltpu.CompilerParams(
            collective_id=0, has_side_effects=True, vmem_limit_bytes=44 * 1024 * 1024),
        cost_estimate=pl.CostEstimate(flops=5_000_000_000, bytes_accessed=4_000_000, transcendentals=0),
    )(ancestor_inverse, factor_panel, pivot_inverse, sn_size, anc_list)


def solution(mesh):
    return jax.shard_map(
        per_device,
        mesh=mesh,
        in_specs=(P("prow", "pcol"), P("prow", "pcol"), P("prow", "pcol"), P(), P()),
        out_specs=(P("pcol", "prow"), P("prow", "pcol")),
        check_vma=False,
    )
```

```python
import jax
import jax.numpy as jnp
from jax import lax
from jax.experimental import pallas as pl
from jax.experimental.pallas import tpu as pltpu
from jax.sharding import PartitionSpec as P

AB = 128
W = 512
MESH = pl.DeviceIdType.MESH
MCH = 4
JOF = (1, 3, 2, 0)
LANE = (3, 0, 2, 1)


def kernel(
    a_ref, l_ref, piv_ref, sn_ref, anc_ref, out_ref, diag_ref,
    abuf, l_in, piv, anc, lhat, spread, lbuf, lead, live, acc, cown, csend, crecv, abf, corr, drecv,
    ld_sem, in_sem, s1_s, s1_r, s2_s, s2_r, s3_s, s3_r, a_s, a_r, ab_r, c_s, c_r, h_s, h_r, d_s, d_r,
):
    rows = l_ref.shape[0]
    mrows = rows // MCH
    half = rows // 2
    quart = half // 4
    kw = a_ref.shape[1]
    tiles = mrows // AB
    p = lax.axis_index("prow")
    q = lax.axis_index("pcol")
    x, zh = p % 4, p // 4
    y, zl, c = q // 8, (q // 2) % 4, q % 2
    z = zh * 4 + zl
    k = q // 4

    def dev(x_, y_, z_, c_):
        return ((z_ // 4) * 4 + x_, y_ * 8 + (z_ % 4) * 2 + c_)

    def at_x(d):
        return dev((x + d) % 4, y, z, c)

    def at_y(d):
        return dev(x, (y + d) % 4, z, c)

    def at_z(z_):
        return dev(x, y, z_, c)

    sib = dev(x, y, z, 1 - c)

    def rcopy(src, dst, ssem, rsem, device):
        return pltpu.make_async_remote_copy(
            src_ref=src, dst_ref=dst, send_sem=ssem, recv_sem=rsem,
            device_id=device, device_id_type=MESH)

    barrier = pltpu.get_barrier_semaphore()
    partners = [at_z((z + d) % 8) for d in range(1, 8)]
    partners += [dev((x + d) % 4, y, ((zh + e) % 2) * 4 + zl, c)
                 for d in range(1, 4) for e in range(2)]
    partners += [at_y(1), at_y(3), sib]
    for partner in partners:
        pl.semaphore_signal(barrier, inc=1, device_id=partner, device_id_type=MESH)

    def mchunk(m):
        return pl.ds(m * mrows, mrows)

    def ablk(y_, c_, r):
        return abuf.at[y_, r, pl.ds(pl.multiple_of(c_ * kw, 128), kw)]

    def load(m):
        r = mchunk(m)
        return pltpu.make_async_copy(a_ref.at[r, :], ablk(y, c, r), ld_sem.at[m])

    l_load = pltpu.make_async_copy(l_ref, l_in, in_sem.at[0])
    anc_load = pltpu.make_async_copy(anc_ref, anc, in_sem.at[1])
    piv_load = pltpu.make_async_copy(piv_ref, piv, in_sem.at[2])
    l_load.start()
    anc_load.start()
    for m in range(MCH):
        load(m).start()
    piv_load.start()

    l_load.wait()
    anc_load.wait()
    ids = p * (rows // AB) + lax.broadcasted_iota(jnp.int32, (16, anc_ref.shape[1]), 0)
    hit = jnp.where(ids == anc[pl.ds(k, 1), :], 1.0, 0.0)
    row_live = jnp.max(hit, axis=1, keepdims=True)
    cols = (q % 4) * AB + lax.broadcasted_iota(jnp.int32, (1, AB), 1)
    col_live = jnp.where(cols < sn_ref[k], 1.0, 0.0)
    live[...] = row_live * col_live
    for b in range(rows // AB):
        r = pl.ds(b * AB, AB)
        lhat[r, :] = (l_in[r, :].astype(jnp.float32) * live[b:b + 1, :]).astype(jnp.bfloat16)
    for h in range(2):
        mine = pl.ds(pl.multiple_of(h * half + x * quart, 64), quart)
        spread[x % 2, h, x // 2] = lhat[mine, :]

    pl.semaphore_wait(barrier, len(partners))

    def s1(d, h):
        s = (x + d) % 4
        return rcopy(lhat.at[pl.ds(pl.multiple_of(h * half + s * quart, 64), quart), :],
                     spread.at[x % 2, h, x // 2], s1_s.at[d - 1, h], s1_r.at[d - 1, h], at_x(d))

    for d in (1, 3, 2):
        for h in range(2):
            s1(d, h).start()

    def a_own(m):
        r = mchunk(m)
        blk = ablk(y, c, r)
        return [rcopy(blk, blk, a_s.at[m, 0], a_r.at[m, 0], at_y(1)),
                rcopy(blk, blk, a_s.at[m, 1], a_r.at[m, 1], at_y(3)),
                rcopy(blk, blk, a_s.at[m, 2], ab_r.at[m, 0], sib)]

    hr = mrows // 2
    ym, yp, yo = (y + 3) % 4, (y + 1) % 4, (y + 2) % 4

    def a_fwd(m):
        lo, hi = pl.ds(m * mrows, hr), pl.ds(m * mrows + hr, hr)
        r = mchunk(m)
        return [rcopy(ablk(ym, c, lo), ablk(ym, c, lo), a_s.at[m, 3], a_r.at[m, 2], at_y(1)),
                rcopy(ablk(yp, c, hi), ablk(yp, c, hi), a_s.at[m, 4], a_r.at[m, 3], at_y(3)),
                rcopy(ablk(ym, c, r), ablk(ym, c, r), a_s.at[m, 5], ab_r.at[m, 1], sib),
                rcopy(ablk(yp, c, r), ablk(yp, c, r), a_s.at[m, 6], ab_r.at[m, 2], sib)]

    def a_opp(m):
        lo, hi = pl.ds(m * mrows, hr), pl.ds(m * mrows + hr, hr)
        return [rcopy(ablk(yo, c, lo), ablk(yo, c, lo), a_s.at[m, 7], ab_r.at[m, 3], sib),
                rcopy(ablk(yo, c, hi), ablk(yo, c, hi), a_s.at[m, 8], ab_r.at[m, 4], sib)]

    def wait_into(ref, sem):
        pltpu.make_async_copy(ref, ref, sem).wait()

    def own_send(m):
        load(m).wait()
        for cp in a_own(m):
            cp.start()

    def relay_a(m):
        r = mchunk(m)
        cps = a_fwd(m)
        wait_into(ablk(ym, c, r), a_r.at[m, 0])
        cps[0].start()
        cps[2].start()
        wait_into(ablk(yp, c, r), a_r.at[m, 1])
        cps[1].start()
        cps[3].start()

    def finish_a(m):
        r = mchunk(m)
        lo, hi = pl.ds(m * mrows, hr), pl.ds(m * mrows + hr, hr)
        cps = a_opp(m)
        wait_into(ablk(yo, c, lo), a_r.at[m, 2])
        cps[0].start()
        wait_into(ablk(yo, c, hi), a_r.at[m, 3])
        cps[1].start()

    def wait_a(m):
        r = mchunk(m)
        lo, hi = pl.ds(m * mrows, hr), pl.ds(m * mrows + hr, hr)
        oc = 1 - c
        wait_into(ablk(y, oc, r), ab_r.at[m, 0])
        wait_into(ablk(ym, oc, r), ab_r.at[m, 1])
        wait_into(ablk(yp, oc, r), ab_r.at[m, 2])
        wait_into(ablk(yo, oc, lo), ab_r.at[m, 3])
        wait_into(ablk(yo, oc, hi), ab_r.at[m, 4])

    own_send(0)
    own_send(1)

    def lanes(d):
        return pl.ds(LANE[d % 4] * AB, AB)

    def s2(d):
        tz = ((z + d) % 8) % 4
        src = spread.at[tz // 2, tz % 2]
        dst = lbuf.at[pl.ds(zh * 2, 2), pl.ds(pl.multiple_of(x * quart, 64), quart), lanes(8 - d)]
        if d == 0:
            return pltpu.make_async_copy(src, dst, s2_r.at[0])
        return rcopy(src, dst, s2_s.at[d], s2_r.at[(8 - d) % 8], at_z((z + d) % 8))

    for h in range(2):
        for d in (1, 3, 2):
            xf = (x + 4 - d) % 4
            wait_into(spread.at[xf % 2, h, xf // 2], s1_r.at[d - 1, h])
    for d in (7, 3, 1, 5, 6, 2, 4, 0):
        s2(d).start()

    def piece(d, s):
        zs = (z + d) % 8
        return lbuf.at[pl.ds((zs // 4) * 2, 2), pl.ds(pl.multiple_of(s * quart, 64), quart), lanes(d)]

    def piece1(d, s, xs):
        zs = (z + d) % 8
        return lbuf.at[(zs // 4) * 2 + xs, pl.ds(pl.multiple_of(s * quart, 64), quart), lanes(d)]

    xm, xp, xo = (x + 3) % 4, (x + 1) % 4, (x + 2) % 4

    def s3(d):
        return [rcopy(piece(d, x), piece(d, x), s3_s.at[d, 0], s3_r.at[d, 0], at_x(1)),
                rcopy(piece(d, x), piece(d, x), s3_s.at[d, 1], s3_r.at[d, 1], at_x(3))]

    def s3_relay(d):
        return [rcopy(piece1(d, xm, 0), piece1(d, xm, 0), s3_s.at[d, 2], s3_r.at[d, 2], at_x(1)),
                rcopy(piece1(d, xp, 1), piece1(d, xp, 1), s3_s.at[d, 3], s3_r.at[d, 3], at_x(3))]

    GROUPS = ((1, 5), (7, 3), (2, 6), (0, 4))

    def spread_x(g):
        for d in GROUPS[g]:
            wait_into(piece(d, x), s2_r.at[d])
            for cp in s3(d):
                cp.start()

    def relay_x(g):
        for d in GROUPS[g]:
            cps = s3_relay(d)
            wait_into(piece(d, xm), s3_r.at[d, 0])
            cps[0].start()
            wait_into(piece(d, xp), s3_r.at[d, 1])
            cps[1].start()

    def wait_x(g):
        for d in GROUPS[g]:
            wait_into(piece1(d, xo, 0), s3_r.at[d, 2])
            wait_into(piece1(d, xo, 1), s3_r.at[d, 3])

    zmate = z + 1 - 2 * (z % 2)

    def hblk(zb, cb):
        return lead.at[:, pl.ds(pl.multiple_of(((zb % 2) * 2 + cb) * AB, 128), AB)]

    h_own = [rcopy(lhat, hblk(z, c), h_s.at[0], h_r.at[0], at_z(zmate)),
             rcopy(lhat, hblk(z, c), h_s.at[1], h_r.at[1], sib)]
    h_fwd = rcopy(hblk(zmate, c), hblk(zmate, c), h_s.at[2], h_r.at[2], sib)
    h_loc = pltpu.make_async_copy(lhat, hblk(z, c), h_s.at[3])

    def c_copy(m, n):
        return rcopy(csend.at[m, n], crecv.at[m, n], c_s.at[m, n], c_r.at[m, n],
                     at_z(zh * 4 + (zl + JOF[n]) % 4))

    def compute(m, n0, n1):
        r = mchunk(m)
        ln = pl.ds(n0 * AB, (n1 - n0) * AB)
        acc[:, ln] = jnp.dot(abuf[0, r, :], lbuf[0, :, ln], preferred_element_type=jnp.float32)
        for yy in range(1, 4):
            acc[:, ln] += jnp.dot(abuf[yy, r, :], lbuf[yy, :, ln], preferred_element_type=jnp.float32)
        for n in range(n0, n1):
            if JOF[n] == 0:
                cown[r, :] = acc[:, n * AB:(n + 1) * AB]
                continue
            for t in range(tiles):
                part = acc[t * AB:(t + 1) * AB, n * AB:(n + 1) * AB]
                top = jnp.max(jnp.abs(part), axis=0, keepdims=True)
                e = jnp.clip(jnp.floor(jnp.log2(jnp.maximum(top, 1e-30))) + 1.0, -90.0, 90.0)
                v = jnp.clip(jnp.round(part * jnp.exp2(15.0 - e)), -32767.0, 32767.0)
                csend[m, n, t, 0:AB, :] = v.astype(jnp.int32).astype(jnp.int16)
                csend[m, n, t, AB:AB + 16, :] = jnp.broadcast_to(
                    e.astype(jnp.int32), (16, AB)).astype(jnp.int16)
            c_copy(m, n).start()

    spread_x(0)
    relay_a(0)
    own_send(2)
    spread_x(1)
    relay_x(0)
    spread_x(2)
    relay_x(1)
    finish_a(0)
    relay_a(1)
    own_send(3)
    spread_x(3)
    h_loc.start()
    for cp in h_own:
        cp.start()
    relay_x(2)
    wait_x(0)
    wait_x(1)
    wait_a(0)
    compute(0, 0, 2)
    relay_x(3)
    finish_a(1)
    wait_a(1)
    compute(1, 0, 2)
    relay_a(2)
    wait_x(2)
    wait_x(3)
    compute(0, 2, 4)
    compute(1, 2, 4)
    relay_a(3)
    finish_a(2)
    wait_a(2)
    compute(2, 0, 4)
    wait_into(hblk(zmate, c), h_r.at[0])
    h_fwd.start()
    finish_a(3)
    wait_a(3)
    compute(3, 0, 4)
    h_loc.wait()
    wait_into(hblk(z, 1 - c), h_r.at[1])
    wait_into(hblk(zmate, 1 - c), h_r.at[2])

    for m in range(MCH):
        for n in range(3):
            wait_into(crecv.at[m, n], c_r.at[m, n])
        for t in range(tiles):
            at = m * mrows + t * AB
            s = cown[at:at + AB, :]
            for n in range(3):
                v = crecv[m, n, t, 0:AB, :].astype(jnp.int32).astype(jnp.float32)
                e = crecv[m, n, t, AB:AB + 16, :].astype(jnp.int32).astype(jnp.float32)
                s = s + v * jnp.exp2(e[0:1, :] - 15.0)
            b = m * tiles + t
            s = -(s * live[b:b + 1, :])
            abf[t * AB:(t + 1) * AB, :] = s.astype(jnp.bfloat16)
            out_ref[:, at:at + AB] = s.T.astype(jnp.bfloat16)
        part = lax.dot_general(
            lead[mchunk(m), :], abf[...], (((0,), (0,)), ((), ())), preferred_element_type=jnp.float32)
        corr[...] = part if m == 0 else corr[...] + part

    lrows = diag_ref.shape[0]

    def mine(p_):
        return pl.ds(pl.multiple_of(p_ * lrows, lrows), lrows)

    dcopies = []
    for d in range(1, 8):
        to = (p + d) % 8
        cp = rcopy(corr.at[mine(to), :], drecv.at[d - 1], d_s.at[d - 1], d_r.at[d - 1], (to, q))
        cp.start()
        dcopies.append(cp)
    total = corr[mine(p), :]
    for d in range(1, 8):
        wait_into(drecv.at[d - 1], d_r.at[d - 1])
        total = total + drecv[d - 1]
    lead_id = p * lrows + lax.broadcasted_iota(jnp.int32, (lrows, AB), 0)
    keep = jnp.where(lead_id < sn_ref[k], 1.0, 0.0) * col_live
    piv_load.wait()
    diag_ref[...] = (piv[...] - total) * keep

    for d in range(1, 4):
        for h in range(2):
            s1(d, h).wait_send()
    for d in range(8):
        if d:
            s2(d).wait_send()
        for cp in s3(d) + s3_relay(d):
            cp.wait_send()
    for m in range(MCH):
        for cp in a_own(m) + a_fwd(m) + a_opp(m):
            cp.wait_send()
        for n in range(3):
            c_copy(m, n).wait_send()
    for cp in h_own + [h_fwd] + dcopies:
        cp.wait_send()


def per_device(ancestor_inverse, factor_panel, pivot_inverse, sn_size, anc_list):
    rows, cols = factor_panel.shape
    kw = ancestor_inverse.shape[1]
    lrows = pivot_inverse.shape[0]
    mrows = rows // MCH
    tiles = mrows // AB
    vm, dma = pltpu.VMEM, pltpu.SemaphoreType.DMA
    bf, f32 = jnp.bfloat16, jnp.float32
    anys = pl.BlockSpec(memory_space=pl.ANY)
    vspec = pl.BlockSpec(memory_space=pltpu.VMEM)
    return pl.pallas_call(
        kernel,
        out_shape=(jax.ShapeDtypeStruct((cols, rows), bf),
                   jax.ShapeDtypeStruct((lrows, cols), f32)),
        in_specs=[anys, anys, anys, pl.BlockSpec(memory_space=pltpu.SMEM), anys],
        out_specs=(vspec, vspec),
        scratch_shapes=[
            vm((4, rows, 2 * kw), bf),
            vm((rows, cols), bf),
            vm((lrows, cols), f32),
            vm(anc_list.shape, jnp.int32),
            vm((rows, cols), bf),
            vm((2, 2, 2, rows // 8, cols), bf),
            vm((4, 2 * kw, 4 * cols), bf),
            vm((rows, W), bf),
            vm((16, cols), f32),
            vm((mrows, 4 * cols), f32),
            vm((rows, cols), f32),
            vm((MCH, 3, tiles, AB + 16, cols), jnp.int16),
            vm((MCH, 3, tiles, AB + 16, cols), jnp.int16),
            vm((mrows, cols), bf),
            vm((W, cols), f32),
            vm((7, lrows, cols), f32),
            dma((MCH,)), dma((3,)), dma((3, 2)), dma((3, 2)),
            dma((8,)), dma((8,)), dma((8, 4)), dma((8, 4)),
            dma((MCH, 9)), dma((MCH, 4)), dma((MCH, 5)),
            dma((MCH, 3)), dma((MCH, 3)),
            dma((4,)), dma((3,)), dma((7,)), dma((7,)),
        ],
        compiler_params=pltpu.CompilerParams(
            collective_id=0, has_side_effects=True, vmem_limit_bytes=60 * 1024 * 1024),
        cost_estimate=pl.CostEstimate(flops=5_000_000_000, bytes_accessed=4_000_000, transcendentals=0),
    )(ancestor_inverse, factor_panel, pivot_inverse, sn_size, anc_list)


def solution(mesh):
    return jax.shard_map(
        per_device,
        mesh=mesh,
        in_specs=(P("prow", "pcol"), P("prow", "pcol"), P("prow", "pcol"), P(), P()),
        out_specs=(P("pcol", "prow"), P("prow", "pcol")),
        check_vma=False,
    )
```

```python
import jax
import jax.numpy as jnp
from jax import lax
from jax.experimental import pallas as pl
from jax.experimental.pallas import tpu as pltpu
from jax.sharding import PartitionSpec as P

AB = 128
W = 512
MESH = pl.DeviceIdType.MESH
CHUNKS = (3, 3, 3, 2, 1)
MCH = len(CHUNKS)
TOP = max(CHUNKS)
JOF = (1, 3, 2, 0)
LANE = (3, 0, 2, 1)


def kernel(
    a_ref, l_ref, piv_ref, sn_ref, anc_ref, out_ref, diag_ref,
    abuf, l_in, piv, anc, lhat, away, lbuf, lead, live, acc, cown, csend, crecv, ckeep, tot, abf, corr, dsend, drecv, out_v, diag_v,
    in_sem, s_s, x_r, s2_r, s3_r, a_r, ab_r, c_r, h_r, out_s,
):
    rows = l_ref.shape[0]
    half = rows // 2
    quart = half // 4
    kw = a_ref.shape[1]
    first = [sum(CHUNKS[:m]) * AB for m in range(MCH)]
    p = lax.axis_index("prow")
    q = lax.axis_index("pcol")
    x, zh = p % 4, p // 4
    y, zl, c = q // 8, (q // 2) % 4, q % 2
    z = zh * 4 + zl
    k = q // 4

    def dev(x_, y_, z_, c_):
        return ((z_ // 4) * 4 + x_, y_ * 8 + (z_ % 4) * 2 + c_)

    def at_x(d):
        return dev((x + d) % 4, y, z, c)

    def at_y(d):
        return dev(x, (y + d) % 4, z, c)

    def at_z(z_):
        return dev(x, y, z_, c)

    sib = dev(x, y, z, 1 - c)

    def rcopy(src, dst, ssem, rsem, device):
        return pltpu.make_async_remote_copy(
            src_ref=src, dst_ref=dst, send_sem=ssem, recv_sem=rsem,
            device_id=device, device_id_type=MESH)

    barrier = pltpu.get_barrier_semaphore()
    partners = [at_z((z + d) % 8) for d in range(1, 8)]
    partners += [dev((x + d) % 4, y, ((zh + e) % 2) * 4 + zl, c)
                 for d in range(1, 4) for e in range(2)]
    partners += [at_y(1), at_y(3), sib]
    for partner in partners:
        pl.semaphore_signal(barrier, inc=1, device_id=partner, device_id_type=MESH)

    def mchunk(m):
        return pl.ds(first[m], CHUNKS[m] * AB)

    def mhalves(m):
        n = CHUNKS[m] * AB // 2
        return pl.ds(first[m], n), pl.ds(first[m] + n, n)

    def ablk(y_, c_, r):
        return abuf.at[y_, r, pl.ds(pl.multiple_of(c_ * kw, 128), kw)]

    a_load = pltpu.make_async_copy(a_ref, ablk(y, c, pl.ds(0, rows)), in_sem.at[3])
    l_load = pltpu.make_async_copy(l_ref, l_in, in_sem.at[0])
    anc_load = pltpu.make_async_copy(anc_ref, anc, in_sem.at[1])
    piv_load = pltpu.make_async_copy(piv_ref, piv, in_sem.at[2])
    l_load.start()
    anc_load.start()
    a_load.start()
    piv_load.start()

    l_load.wait()
    anc_load.wait()
    ids = p * (rows // AB) + lax.broadcasted_iota(jnp.int32, (16, anc_ref.shape[1]), 0)
    hit = jnp.where(ids == anc[pl.ds(k, 1), :], 1.0, 0.0)
    row_live = jnp.max(hit, axis=1, keepdims=True)
    cols = (q % 4) * AB + lax.broadcasted_iota(jnp.int32, (1, AB), 1)
    col_live = jnp.where(cols < sn_ref[k], 1.0, 0.0)
    live[...] = row_live * col_live
    for b in range(rows // AB):
        r = pl.ds(b * AB, AB)
        w = (l_in[r, :].astype(jnp.float32) * live[b:b + 1, :]).astype(jnp.bfloat16)
        lhat[b * AB // half, pl.ds(b * AB % half, AB), :] = w

    pl.semaphore_wait(barrier, len(partners))

    s1 = [rcopy(lhat.at[:, pl.ds((2 + i) * quart, quart), :], away.at[i], s_s.at[0], x_r.at[0], at_x(1 + 2 * i))
          for i in range(2)]
    for cp in s1:
        cp.start()

    def lanes(d):
        return pl.ds(LANE[d % 4] * AB, AB)

    def place(x_, zl_, zh_, i):
        home = 1 - (x_ + zl_ // 2) % 2
        xs = home * (x_ // 2) + (1 - home) * (((x_ + 3 + 2 * i) % 4) // 2)
        row = (1 - home) * 2 * quart + i * quart
        return zh_ * 2 + xs, pl.ds(pl.multiple_of(row, 64), quart)

    def s2(d, i, home):
        tz = (z + d) % 4
        src = lhat.at[tz % 2, pl.ds(i * quart, quart), :] if home else away.at[i, tz % 2]
        blk, row = place(x, tz, zh, i)
        dst = lbuf.at[blk, row, lanes(8 - d)]
        sem = s2_r.at[(8 - d) % 8]
        if d == 0:
            return pltpu.make_async_copy(src, dst, sem)
        return rcopy(src, dst, s_s.at[1], sem, at_z((z + d) % 8))

    S2_ORDER = ((7, 3), (1, 5), (6, 2), (4, 0))
    homes = [1 - (x + ((z + g[0]) % 4) // 2) % 2 for g in S2_ORDER]
    first_home = [homes[0], (1 - homes[0]) * homes[1], (1 - homes[0]) * (1 - homes[1]), 0]
    first_away = [1 - homes[0], homes[0] * (1 - homes[1]), homes[0] * homes[1], 0]

    def s2_start(when, home):
        for g, cond in zip(S2_ORDER, when):
            @pl.when(cond == 1)
            def _(g=g):
                for d in g:
                    for i in range(2):
                        s2(d, i, home).start()

    s2_start(first_home, True)

    zmate = z + 1 - 2 * (z % 2)

    def hblk(zb, cb):
        return lead.at[:, :, pl.ds(pl.multiple_of(((zb % 2) * 2 + cb) * AB, 128), AB)]

    h_own = [rcopy(lhat, hblk(z, c), s_s.at[4], h_r.at[0], at_z(zmate)),
             rcopy(lhat, hblk(z, c), s_s.at[4], h_r.at[1], sib)]
    h_fwd = rcopy(hblk(zmate, c), hblk(zmate, c), s_s.at[4], h_r.at[1], sib)
    h_loc = pltpu.make_async_copy(lhat, hblk(z, c), h_r.at[2])

    def send_lead():
        h_loc.start()
        for cp in h_own:
            cp.start()

    def a_own(m):
        r = mchunk(m)
        blk = ablk(y, c, r)
        return [rcopy(blk, blk, s_s.at[3], a_r.at[m, 0], at_y(1)),
                rcopy(blk, blk, s_s.at[3], a_r.at[m, 0], at_y(3)),
                rcopy(blk, blk, s_s.at[3], ab_r.at[m], sib)]

    ym, yp, yo = (y + 3) % 4, (y + 1) % 4, (y + 2) % 4

    def a_fwd(m):
        lo, hi = mhalves(m)
        r = mchunk(m)
        return [rcopy(ablk(ym, c, lo), ablk(ym, c, lo), s_s.at[3], a_r.at[m, 1], at_y(1)),
                rcopy(ablk(yp, c, hi), ablk(yp, c, hi), s_s.at[3], a_r.at[m, 1], at_y(3)),
                rcopy(ablk(ym, c, r), ablk(ym, c, r), s_s.at[3], ab_r.at[m], sib),
                rcopy(ablk(yp, c, r), ablk(yp, c, r), s_s.at[3], ab_r.at[m], sib)]

    def a_opp(m):
        r = mchunk(m)
        return [rcopy(ablk(yo, c, r), ablk(yo, c, r), s_s.at[3], ab_r.at[m], sib)]

    def wait_into(ref, sem):
        pltpu.make_async_copy(ref, ref, sem).wait()

    def own_send(m):
        for cp in a_own(m):
            cp.start()

    def relay_a(m):
        wait_into(abuf.at[pl.ds(0, 2), mchunk(m), pl.ds(0, kw)], a_r.at[m, 0])
        for cp in a_fwd(m):
            cp.start()

    def finish_a(m):
        wait_into(abuf.at[0, mchunk(m), pl.ds(0, kw)], a_r.at[m, 1])
        for cp in a_opp(m):
            cp.start()

    def wait_a(m):
        wait_into(abuf.at[:, mchunk(m), pl.ds(0, kw)], ab_r.at[m])

    a_load.wait()
    own_send(0)
    own_send(1)
    own_send(2)

    wait_into(away, x_r.at[0])
    s2_start(first_away, False)
    s2_start([h - f for h, f in zip(homes, first_home)], True)
    s2_start([1 - h - f for h, f in zip(homes, first_away)], False)

    def piece(d, x_, i):
        blk, row = place(x_, zl, ((z + d) % 8) // 4, i)
        return lbuf.at[blk, row, lanes(d)]

    xm, xp, xo = (x + 3) % 4, (x + 1) % 4, (x + 2) % 4

    def s3(d, i):
        return [rcopy(piece(d, x, i), piece(d, x, i), s_s.at[2], s3_r.at[d, 0], at_x(1)),
                rcopy(piece(d, x, i), piece(d, x, i), s_s.at[2], s3_r.at[d, 1], at_x(3))]

    def s3_relay(d):
        return [rcopy(piece(d, xm, 0), piece(d, xm, 0), s_s.at[2], s3_r.at[d, 2], at_x(1)),
                rcopy(piece(d, xp, 1), piece(d, xp, 1), s_s.at[2], s3_r.at[d, 2], at_x(3))]

    GROUPS = ((1, 5), (7, 3), (2, 6), (0, 4))

    def wait_pair(sem):
        wait_into(lbuf.at[pl.ds(0, 2), pl.ds(0, quart), pl.ds(0, AB)], sem)

    def spread_x(g):
        for d in GROUPS[g]:
            wait_pair(s2_r.at[d])
            for i in range(2):
                for cp in s3(d, i):
                    cp.start()

    def relay_x(g):
        for d in GROUPS[g]:
            cps = s3_relay(d)
            wait_pair(s3_r.at[d, 0])
            cps[0].start()
            wait_pair(s3_r.at[d, 1])
            cps[1].start()

    def wait_x(g):
        for d in GROUPS[g]:
            wait_pair(s3_r.at[d, 2])

    is_end = zl * (3 - zl) == 0
    at_hi, at_lo = (zl + 1) // 4, (4 - zl) // 4

    def cout(m, n):
        return csend.at[n, pl.ds(first[m] + 16 * m, 16 + CHUNKS[m] * AB)]

    def c_copy(m, n):
        if n == 0:
            to, slot = zl + 1 - 2 * at_hi, 3 * at_hi
        elif n == 1:
            to, slot = zl - 1 + 2 * at_lo, 1 + 2 * at_lo
        else:
            to, slot = (zl + 2) % 4, 2
        t = pl.ds(0, 16 + CHUNKS[m] * AB)
        return rcopy(cout(m, n), crecv.at[m, slot, t], s_s.at[5], c_r.at[m, slot], at_z(zh * 4 + to))

    def code(part, dst, step=AB):
        n = part.shape[0]
        at = lax.broadcasted_iota(jnp.int32, (16, AB), 0)
        powers = jnp.zeros((16, AB), jnp.float32)
        for t in range(n // step):
            b = part[t * step:(t + 1) * step, :]
            top = jnp.max(jnp.abs(b), axis=0, keepdims=True)
            e = jnp.clip(jnp.floor(jnp.log2(jnp.maximum(top, 1e-30))) + 1.0, -90.0, 90.0)
            v = jnp.clip(jnp.round(b * jnp.exp2(15.0 - e)), -32767.0, 32767.0)
            dst[16 + t * step:16 + (t + 1) * step, :] = v.astype(jnp.int32).astype(jnp.int16)
            powers = jnp.where(at == t, e, powers)
        dst[0:16, :] = powers.astype(jnp.int32).astype(jnp.int16)

    def decode(src, t=0, step=AB):
        v = src[16 + t * step:16 + (t + 1) * step, :].astype(jnp.int32).astype(jnp.float32)
        e = src[0:16, :].astype(jnp.int32).astype(jnp.float32)
        return v * jnp.exp2(e[t:t + 1, :] - 15.0)

    def compute(m, n0, n1):
        r = mchunk(m)
        n = CHUNKS[m] * AB
        ln = pl.ds(n0 * AB, (n1 - n0) * AB)
        acc[0:n, ln] = jnp.dot(abuf[0, r, :], lbuf[0, :, ln], preferred_element_type=jnp.float32)
        for yy in range(1, 4):
            acc[0:n, ln] += jnp.dot(abuf[yy, r, :], lbuf[yy, :, ln], preferred_element_type=jnp.float32)
        for b in range(n0, n1):
            part = acc[0:n, b * AB:(b + 1) * AB]
            if b == 3:
                cown[r, :] = part
            elif b == 2:
                ckeep[m, 0:n, :] = part
                pl.when(is_end)(lambda: send_far(m))
            else:
                code(part, cout(m, b))
                c_copy(m, b).start()

    def send_far(m):
        code(ckeep[m, 0:CHUNKS[m] * AB, :], cout(m, 2))
        c_copy(m, 2).start()

    def wait_c(m, slot):
        wait_into(crecv.at[m, slot, pl.ds(0, 16 + CHUNKS[m] * AB)], c_r.at[m, slot])

    def merge(m):
        @pl.when(jnp.logical_not(is_end))
        def _():
            wait_c(m, 3)
            for t in range(CHUNKS[m]):
                ckeep[m, t * AB:(t + 1) * AB, :] += decode(crecv.at[m, 3], t)
            code(ckeep[m, 0:CHUNKS[m] * AB, :], cout(m, 2))
            c_copy(m, 2).start()

    def add_slot(m, n):
        wait_c(m, n)
        for t in range(CHUNKS[m]):
            tot[t * AB:(t + 1) * AB, :] += decode(crecv.at[m, n], t)

    def out_copy(m):
        return pltpu.make_async_copy(out_v.at[:, mchunk(m)], out_ref.at[:, mchunk(m)], out_s.at[0])

    def finish_c(m):
        n = CHUNKS[m] * AB
        tot[0:n, :] = cown[mchunk(m), :]
        pl.when(zl >= 1)(lambda: add_slot(m, 0))
        pl.when(zl <= 2)(lambda: add_slot(m, 1))
        add_slot(m, 2)
        for t in range(CHUNKS[m]):
            at = first[m] + t * AB
            b = at // AB
            v = -(tot[t * AB:(t + 1) * AB, :] * live[b:b + 1, :])
            abf[t * AB:(t + 1) * AB, :] = v.astype(jnp.bfloat16)
            out_v[:, at:at + AB] = v.T.astype(jnp.bfloat16)
        out_copy(m).start()
        part = lax.dot_general(
            lead[first[m] // half, pl.ds(first[m] % half, n), :], abf[0:n, :],
            (((0,), (0,)), ((), ())), preferred_element_type=jnp.float32)
        corr[...] = part if m == 0 else corr[...] + part

    def wait_lead():
        h_loc.wait()
        wait_into(lead.at[:, :, pl.ds(0, 2 * AB)], h_r.at[1])

    def fwd_lead():
        wait_into(hblk(zmate, c), h_r.at[0])
        h_fwd.start()

    def sent():
        wait_into(away, s_s.at[0])
        wait_into(abuf.at[0, pl.ds(0, 14 * quart * AB // (2 * kw)), :], s_s.at[1])
        wait_into(abuf.at[0], s_s.at[2])
        wait_into(abuf.at[:, pl.ds(0, rows * 7 // 8), :], s_s.at[3])
        wait_into(lead.at[:, :, pl.ds(0, 3 * AB)], s_s.at[4])

    spread_x(0)
    relay_a(0)
    spread_x(1)
    relay_x(0)
    relay_a(1)
    own_send(3)
    own_send(4)
    relay_x(1)
    spread_x(2)
    spread_x(3)
    send_lead()
    relay_a(2)
    finish_a(0)
    wait_x(0)
    wait_x(1)
    wait_a(0)
    compute(0, 0, 2)
    relay_x(2)
    finish_a(1)
    wait_a(1)
    compute(1, 0, 2)
    relay_x(3)
    relay_a(3)
    wait_x(2)
    wait_x(3)
    compute(0, 2, 4)
    relay_a(4)
    fwd_lead()
    compute(1, 2, 4)
    finish_a(2)
    merge(0)
    wait_a(2)
    compute(2, 0, 4)
    finish_a(3)
    merge(1)
    finish_a(4)
    wait_a(3)
    compute(3, 0, 4)
    wait_a(4)
    compute(4, 0, 4)
    wait_lead()
    merge(2)
    sent()
    finish_c(0)
    merge(3)
    finish_c(1)
    merge(4)
    finish_c(2)
    finish_c(3)
    finish_c(4)
    wait_into(csend, s_s.at[5])

    lrows = diag_ref.shape[0]

    def mine(p_):
        return pl.ds(pl.multiple_of(p_ * lrows, lrows), lrows)

    for d in (4, 1, 3, 2, 5, 7, 6):
        to = (zh + d // 4) % 2 * 4 + (x + d) % 4
        code(corr[mine(to), :], dsend.at[d - 1], lrows)
        cp = rcopy(dsend.at[d - 1], drecv.at[d - 1], s_s.at[6], x_r.at[1], (to, q))
        cp.start()
    total = corr[mine(p), :]
    wait_into(drecv, x_r.at[1])
    for d in range(1, 8):
        total = total + decode(drecv.at[d - 1], 0, lrows)
    lead_id = p * lrows + lax.broadcasted_iota(jnp.int32, (lrows, AB), 0)
    keep = jnp.where(lead_id < sn_ref[k], 1.0, 0.0) * col_live
    piv_load.wait()
    diag_v[...] = (piv[...] - total) * keep
    diag_copy = pltpu.make_async_copy(diag_v, diag_ref, out_s.at[1])
    diag_copy.start()
    wait_into(dsend, s_s.at[6])
    pltpu.make_async_copy(out_v, out_ref, out_s.at[0]).wait()
    diag_copy.wait()


def per_device(ancestor_inverse, factor_panel, pivot_inverse, sn_size, anc_list):
    rows, cols = factor_panel.shape
    kw = ancestor_inverse.shape[1]
    lrows = pivot_inverse.shape[0]
    vm, dma = pltpu.VMEM, pltpu.SemaphoreType.DMA
    bf, f32 = jnp.bfloat16, jnp.float32
    anys = pl.BlockSpec(memory_space=pl.ANY)
    return pl.pallas_call(
        kernel,
        out_shape=(jax.ShapeDtypeStruct((cols, rows), bf),
                   jax.ShapeDtypeStruct((lrows, cols), f32)),
        in_specs=[anys, anys, anys, pl.BlockSpec(memory_space=pltpu.SMEM), anys],
        out_specs=(anys, anys),
        scratch_shapes=[
            vm((4, rows, 2 * kw), bf),
            vm((rows, cols), bf),
            vm((lrows, cols), f32),
            vm(anc_list.shape, jnp.int32),
            vm((2, rows // 2, cols), bf),
            vm((2, 2, rows // 8, cols), bf),
            vm((4, 2 * kw, 4 * cols), bf),
            vm((2, rows // 2, W), bf),
            vm((16, cols), f32),
            vm((TOP * AB, 4 * cols), f32),
            vm((rows, cols), f32),
            vm((3, rows + 16 * MCH, cols), jnp.int16),
            vm((MCH, 4, 16 + TOP * AB, cols), jnp.int16),
            vm((MCH, TOP * AB, cols), f32),
            vm((TOP * AB, cols), f32),
            vm((TOP * AB, cols), bf),
            vm((W, cols), f32),
            vm((7, lrows + 16, cols), jnp.int16),
            vm((7, lrows + 16, cols), jnp.int16),
            vm((cols, rows), bf),
            vm((lrows, cols), f32),
            dma((4,)), dma((7,)), dma((2,)), dma((8,)), dma((8, 3)),
            dma((MCH, 2)), dma((MCH,)), dma((MCH, 4)), dma((3,)), dma((2,)),
        ],
        compiler_params=pltpu.CompilerParams(
            collective_id=0, has_side_effects=True, vmem_limit_bytes=60 * 1024 * 1024),
        cost_estimate=pl.CostEstimate(flops=5_000_000_000, bytes_accessed=4_000_000, transcendentals=0),
    )(ancestor_inverse, factor_panel, pivot_inverse, sn_size, anc_list)


def solution(mesh):
    return jax.shard_map(
        per_device,
        mesh=mesh,
        in_specs=(P("prow", "pcol"), P("prow", "pcol"), P("prow", "pcol"), P(), P()),
        out_specs=(P("pcol", "prow"), P("prow", "pcol")),
        check_vma=False,
    )
```

```python
import jax
import jax.numpy as jnp
from jax import lax
from jax.experimental import pallas as pl
from jax.experimental.pallas import tpu as pltpu
from jax.sharding import PartitionSpec as P

AB = 128
W = 512
MESH = pl.DeviceIdType.MESH
CHUNKS = (3, 3, 3, 2, 1)
MCH = len(CHUNKS)
TOP = max(CHUNKS)

FIRST = (
    ("spread_x", 0), ("relay_a", 0), ("own_send", 2), ("spread_x", 1), ("relay_x", 0), ("send_lead",), ("relay_a", 1),
    ("own_send", 3), ("own_send", 4), ("relay_x", 1), ("spread_x", 2), ("finish_a", 0), ("relay_a", 2),
)
REST = (
    ("wait_x", 0), ("wait_x", 1), ("spread_x", 3), ("wait_a", 0), ("compute", 0, 0, 2), ("relay_x", 2), ("finish_a", 1),
    ("wait_a", 1), ("compute", 1, 0, 2), ("merge", 0), ("relay_x", 3), ("relay_a", 3), ("relay_a", 4),
    ("wait_x", 2), ("compute", 0, 2, 3), ("finish_a", 2), ("merge", 1), ("fwd_lead",),
    ("wait_x", 3), ("wait_a", 2), ("compute", 2, 0, 4), ("finish_a", 3), ("finish_a", 4),
    ("wait_a", 3), ("compute", 3, 0, 4), ("merge", 2), ("wait_a", 4), ("compute", 4, 0, 4), ("compute", 1, 2, 4), ("compute", 0, 3, 4),
    ("wait_lead",), ("sent",), ("merge", 3), ("finish_c", 0), ("merge", 4),
    ("finish_c", 1), ("finish_c", 2), ("finish_c", 3), ("finish_c", 4),
)


def kernel(
    a_ref, l_ref, piv_ref, sn_ref, anc_ref, out_ref, diag_ref,
    abuf, l_in, piv, anc, lhat, away, lbuf, lead, live, acc, cown, csend, crecv, ckeep, tot, abf, corr, dsend, drecv, out_v, diag_v,
    in_sem, s_s, x_r, s2_r, s3_r, a_r, ab_r, c_r, h_r, out_s,
):
    rows = l_ref.shape[0]
    half = rows // 2
    quart = half // 4
    kw = a_ref.shape[1]
    first = [sum(CHUNKS[:m]) * AB for m in range(MCH)]
    p = lax.axis_index("prow")
    q = lax.axis_index("pcol")
    x, zh = p % 4, p // 4
    y, zl, c = q // 8, (q // 2) % 4, q % 2
    z = zh * 4 + zl
    k = q // 4

    def dev(x_, y_, z_, c_):
        return ((z_ // 4) * 4 + x_, y_ * 8 + (z_ % 4) * 2 + c_)

    other = ((zl + 2) % 4, 3 - zl, zl + 1 - 2 * (zl % 2), zl)

    def at_x(d):
        return dev((x + d) % 4, y, z, c)

    def at_y(d):
        return dev(x, (y + d) % 4, z, c)

    def at_z(z_):
        return dev(x, y, z_, c)

    sib = dev(x, y, z, 1 - c)

    def rcopy(src, dst, ssem, rsem, device):
        return pltpu.make_async_remote_copy(
            src_ref=src, dst_ref=dst, send_sem=ssem, recv_sem=rsem,
            device_id=device, device_id_type=MESH)

    barrier = pltpu.get_barrier_semaphore()
    partners = [at_z((z + d) % 8) for d in range(1, 8)]
    partners += [dev((x + d) % 4, y, ((zh + e) % 2) * 4 + zl, c)
                 for d in range(1, 4) for e in range(2)]
    partners += [at_y(1), at_y(3), sib]
    for partner in partners:
        pl.semaphore_signal(barrier, inc=1, device_id=partner, device_id_type=MESH)

    def mchunk(m):
        return pl.ds(first[m], CHUNKS[m] * AB)

    def mhalves(m):
        n = CHUNKS[m] * AB // 2
        return pl.ds(first[m], n), pl.ds(first[m] + n, n)

    def ablk(y_, c_, r):
        return abuf.at[y_, r, pl.ds(pl.multiple_of(c_ * kw, 128), kw)]

    a_load = pltpu.make_async_copy(a_ref, ablk(y, c, pl.ds(0, rows)), in_sem.at[3])
    l_load = pltpu.make_async_copy(l_ref, l_in, in_sem.at[0])
    anc_load = pltpu.make_async_copy(anc_ref, anc, in_sem.at[1])
    piv_load = pltpu.make_async_copy(piv_ref, piv, in_sem.at[2])
    l_load.start()
    anc_load.start()
    a_load.start()
    piv_load.start()

    l_load.wait()
    anc_load.wait()
    ids = p * (rows // AB) + lax.broadcasted_iota(jnp.int32, (16, anc_ref.shape[1]), 0)
    hit = jnp.where(ids == anc[pl.ds(k, 1), :], 1.0, 0.0)
    row_live = jnp.max(hit, axis=1, keepdims=True)
    cols = (q % 4) * AB + lax.broadcasted_iota(jnp.int32, (1, AB), 1)
    col_live = jnp.where(cols < sn_ref[k], 1.0, 0.0)
    live[...] = row_live * col_live
    for b in range(rows // AB):
        r = pl.ds(b * AB, AB)
        w = (l_in[r, :].astype(jnp.float32) * live[b:b + 1, :]).astype(jnp.bfloat16)
        lhat[b * AB // half, pl.ds(b * AB % half, AB), :] = w

    pl.semaphore_wait(barrier, len(partners))

    s1 = [rcopy(lhat.at[:, pl.ds((2 + i) * quart, quart), :], away.at[i], s_s.at[0], x_r.at[0], at_x(1 + 2 * i))
          for i in range(2)]
    for cp in s1:
        cp.start()

    def lanes(n):
        return pl.ds(n * AB, AB)

    def place(x_, zl_, zh_, i):
        home = 1 - (x_ + zl_ // 2) % 2
        xs = home * (x_ // 2) + (1 - home) * (((x_ + 3 + 2 * i) % 4) // 2)
        row = (1 - home) * 2 * quart + i * quart
        return zh_ * 2 + xs, pl.ds(pl.multiple_of(row, 64), quart)

    def s2(n, e, i, home):
        tz = other[n]
        src = lhat.at[tz % 2, pl.ds(i * quart, quart), :] if home else away.at[i, tz % 2]
        blk, row = place(x, tz, zh, i)
        dst = lbuf.at[blk, row, lanes(n)]
        sem = s2_r.at[2 * n + e]
        if n == 3 and e == 0:
            return pltpu.make_async_copy(src, dst, sem)
        return rcopy(src, dst, s_s.at[1], sem, at_z((zh + e) % 2 * 4 + tz))

    is_home = (x + zl // 2) % 2 == 0
    is_away = (x + zl // 2) % 2 == 1

    def s2_start(cond, home, *blocks):
        @pl.when(cond)
        def _():
            for n in blocks:
                for e in range(2):
                    for i in range(2):
                        s2(n, e, i, home).start()

    s2_start(is_away, True, 0, 1)
    s2_start(is_home, True, 2)

    zmate = z + 1 - 2 * (z % 2)

    def hblk(zb, cb):
        return lead.at[:, :, pl.ds(pl.multiple_of(((zb % 2) * 2 + cb) * AB, 128), AB)]

    h_own = [rcopy(lhat, hblk(z, c), s_s.at[4], h_r.at[0], at_z(zmate)),
             rcopy(lhat, hblk(z, c), s_s.at[4], h_r.at[1], sib)]
    h_fwd = rcopy(hblk(zmate, c), hblk(zmate, c), s_s.at[4], h_r.at[1], sib)
    h_loc = pltpu.make_async_copy(lhat, hblk(z, c), h_r.at[2])

    def send_lead():
        h_loc.start()
        for cp in h_own:
            cp.start()

    def a_own(m):
        r = mchunk(m)
        blk = ablk(y, c, r)
        return [rcopy(blk, blk, s_s.at[3], a_r.at[m, 0], at_y(1)),
                rcopy(blk, blk, s_s.at[3], a_r.at[m, 0], at_y(3)),
                rcopy(blk, blk, s_s.at[3], ab_r.at[m], sib)]

    ym, yp, yo = (y + 3) % 4, (y + 1) % 4, (y + 2) % 4

    def a_fwd(m):
        lo, hi = mhalves(m)
        r = mchunk(m)
        return [rcopy(ablk(ym, c, lo), ablk(ym, c, lo), s_s.at[3], a_r.at[m, 1], at_y(1)),
                rcopy(ablk(yp, c, hi), ablk(yp, c, hi), s_s.at[3], a_r.at[m, 1], at_y(3)),
                rcopy(ablk(ym, c, r), ablk(ym, c, r), s_s.at[3], ab_r.at[m], sib),
                rcopy(ablk(yp, c, r), ablk(yp, c, r), s_s.at[3], ab_r.at[m], sib)]

    def a_opp(m):
        r = mchunk(m)
        return [rcopy(ablk(yo, c, r), ablk(yo, c, r), s_s.at[3], ab_r.at[m], sib)]

    def wait_into(ref, sem):
        pltpu.make_async_copy(ref, ref, sem).wait()

    def own_send(m):
        for cp in a_own(m):
            cp.start()

    def relay_a(m):
        wait_into(abuf.at[pl.ds(0, 2), mchunk(m), pl.ds(0, kw)], a_r.at[m, 0])
        for cp in a_fwd(m):
            cp.start()

    def finish_a(m):
        wait_into(abuf.at[0, mchunk(m), pl.ds(0, kw)], a_r.at[m, 1])
        for cp in a_opp(m):
            cp.start()

    def wait_a(m):
        wait_into(abuf.at[:, mchunk(m), pl.ds(0, kw)], ab_r.at[m])

    a_load.wait()
    own_send(0)
    own_send(1)

    wait_into(away, x_r.at[0])
    s2_start(is_home, False, 0, 1)
    s2_start(is_home, True, 3)
    s2_start(is_away, False, 2, 3)

    def piece(n, e, x_, i):
        blk, row = place(x_, zl, (zh + e) % 2, i)
        return lbuf.at[blk, row, lanes(n)]

    xm, xp, xo = (x + 3) % 4, (x + 1) % 4, (x + 2) % 4

    def s3(n, e, i):
        k = 2 * n + e
        return [rcopy(piece(n, e, x, i), piece(n, e, x, i), s_s.at[2], s3_r.at[k, 0], at_x(1)),
                rcopy(piece(n, e, x, i), piece(n, e, x, i), s_s.at[2], s3_r.at[k, 1], at_x(3))]

    def s3_relay(n, e):
        k = 2 * n + e
        return [rcopy(piece(n, e, xm, 0), piece(n, e, xm, 0), s_s.at[2], s3_r.at[k, 2], at_x(1)),
                rcopy(piece(n, e, xp, 1), piece(n, e, xp, 1), s_s.at[2], s3_r.at[k, 2], at_x(3))]

    def wait_pair(sem):
        wait_into(lbuf.at[pl.ds(0, 2), pl.ds(0, quart), pl.ds(0, AB)], sem)

    def spread_x(n):
        for e in range(2):
            wait_pair(s2_r.at[2 * n + e])
            for i in range(2):
                for cp in s3(n, e, i):
                    cp.start()

    def relay_x(n):
        for e in range(2):
            cps = s3_relay(n, e)
            wait_pair(s3_r.at[2 * n + e, 0])
            cps[0].start()
            wait_pair(s3_r.at[2 * n + e, 1])
            cps[1].start()

    def wait_x(n):
        for e in range(2):
            wait_pair(s3_r.at[2 * n + e, 2])

    is_end = zl * (3 - zl) == 0
    def cout(m, n):
        return csend.at[n, pl.ds(first[m] + 16 * m, 16 + CHUNKS[m] * AB)]

    def c_copy(m, n, far=False):
        to, slot = (other[2], 3) if far else (other[n], n)
        t = pl.ds(0, 16 + CHUNKS[m] * AB)
        return rcopy(cout(m, n), crecv.at[m, slot, t], s_s.at[5], c_r.at[m, slot], at_z(zh * 4 + to))

    def code(part, dst, step=AB):
        n = part.shape[0]
        at = lax.broadcasted_iota(jnp.int32, (16, AB), 0)
        powers = jnp.zeros((16, AB), jnp.float32)
        for t in range(n // step):
            b = part[t * step:(t + 1) * step, :]
            top = jnp.max(jnp.abs(b), axis=0, keepdims=True)
            e = jnp.clip(jnp.floor(jnp.log2(jnp.maximum(top, 1e-30))) + 1.0, -90.0, 90.0)
            v = jnp.clip(jnp.round(b * jnp.exp2(15.0 - e)), -32767.0, 32767.0)
            dst[16 + t * step:16 + (t + 1) * step, :] = v.astype(jnp.int32).astype(jnp.int16)
            powers = jnp.where(at == t, e, powers)
        dst[0:16, :] = powers.astype(jnp.int32).astype(jnp.int16)

    def decode(src, t=0, step=AB):
        v = src[16 + t * step:16 + (t + 1) * step, :].astype(jnp.int32).astype(jnp.float32)
        e = src[0:16, :].astype(jnp.int32).astype(jnp.float32)
        return v * jnp.exp2(e[t:t + 1, :] - 15.0)

    is_inner = zl * (3 - zl) != 0

    def compute(m, n0, n1):
        r = mchunk(m)
        n = CHUNKS[m] * AB
        ln = pl.ds(n0 * AB, (n1 - n0) * AB)
        acc[0:n, ln] = jnp.dot(abuf[0, r, :], lbuf[0, :, ln], preferred_element_type=jnp.float32)
        for yy in range(1, 4):
            acc[0:n, ln] += jnp.dot(abuf[yy, r, :], lbuf[yy, :, ln], preferred_element_type=jnp.float32)
        if n0 == 0:
            code(acc[0:n, AB:2 * AB], cout(m, 1))
            pl.when(is_end)(lambda: c_copy(m, 1, True).start())
            pl.when(is_inner)(lambda: c_copy(m, 1).start())
            ckeep[m, 0:n, :] = acc[0:n, 0:AB]

            @pl.when(is_end)
            def _():
                code(ckeep[m, 0:n, :], cout(m, 0))
                c_copy(m, 0).start()

        if n0 <= 2 < n1:
            code(acc[0:n, 2 * AB:3 * AB], cout(m, 2))
            c_copy(m, 2).start()
        if n1 == 4:
            cown[r, :] = acc[0:n, 3 * AB:4 * AB]

    def wait_c(m, slot):
        wait_into(crecv.at[m, slot, pl.ds(0, 16 + CHUNKS[m] * AB)], c_r.at[m, slot])

    def merge(m):
        @pl.when(is_inner)
        def _():
            wait_c(m, 3)
            for t in range(CHUNKS[m]):
                ckeep[m, t * AB:(t + 1) * AB, :] += decode(crecv.at[m, 3], t)
            code(ckeep[m, 0:CHUNKS[m] * AB, :], cout(m, 0))
            c_copy(m, 0).start()

    def add_slot(m, n):
        wait_c(m, n)
        for t in range(CHUNKS[m]):
            tot[t * AB:(t + 1) * AB, :] += decode(crecv.at[m, n], t)

    def out_copy(m):
        return pltpu.make_async_copy(out_v.at[:, mchunk(m)], out_ref.at[:, mchunk(m)], out_s.at[0])

    def finish_c(m):
        n = CHUNKS[m] * AB
        tot[0:n, :] = cown[mchunk(m), :]
        add_slot(m, 2)
        pl.when(is_inner)(lambda: add_slot(m, 1))
        add_slot(m, 0)
        for t in range(CHUNKS[m]):
            at = first[m] + t * AB
            b = at // AB
            v = -(tot[t * AB:(t + 1) * AB, :] * live[b:b + 1, :])
            abf[t * AB:(t + 1) * AB, :] = v.astype(jnp.bfloat16)
            out_v[:, at:at + AB] = v.T.astype(jnp.bfloat16)
        out_copy(m).start()
        part = lax.dot_general(
            lead[first[m] // half, pl.ds(first[m] % half, n), :], abf[0:n, :],
            (((0,), (0,)), ((), ())), preferred_element_type=jnp.float32)
        corr[...] = part if m == 0 else corr[...] + part

    def wait_lead():
        h_loc.wait()
        wait_into(lead.at[:, :, pl.ds(0, 2 * AB)], h_r.at[1])

    def fwd_lead():
        wait_into(hblk(zmate, c), h_r.at[0])
        h_fwd.start()

    def sent():
        wait_into(away, s_s.at[0])
        wait_into(abuf.at[0, pl.ds(0, 14 * quart * AB // (2 * kw)), :], s_s.at[1])
        wait_into(abuf.at[0], s_s.at[2])
        wait_into(abuf.at[:, pl.ds(0, rows * 7 // 8), :], s_s.at[3])
        wait_into(lead.at[:, :, pl.ds(0, 3 * AB)], s_s.at[4])

    steps = {f.__name__: f for f in (
        spread_x, relay_x, wait_x, own_send, relay_a, finish_a, wait_a, send_lead, fwd_lead, wait_lead,
        compute, merge, sent, finish_c)}

    def run(plan):
        for name, *at in plan:
            steps[name](*at)

    run(FIRST)
    run(REST)
    wait_into(csend, s_s.at[5])

    lrows = diag_ref.shape[0]

    def mine(p_):
        return pl.ds(pl.multiple_of(p_ * lrows, lrows), lrows)

    for d in (4, 1, 3, 2, 5, 7, 6):
        to = (zh + d // 4) % 2 * 4 + (x + d) % 4
        code(corr[mine(to), :], dsend.at[d - 1], lrows)
        cp = rcopy(dsend.at[d - 1], drecv.at[d - 1], s_s.at[6], x_r.at[1], (to, q))
        cp.start()
    total = corr[mine(p), :]
    wait_into(drecv, x_r.at[1])
    for d in range(1, 8):
        total = total + decode(drecv.at[d - 1], 0, lrows)
    lead_id = p * lrows + lax.broadcasted_iota(jnp.int32, (lrows, AB), 0)
    keep = jnp.where(lead_id < sn_ref[k], 1.0, 0.0) * col_live
    piv_load.wait()
    diag_v[...] = (piv[...] - total) * keep
    diag_copy = pltpu.make_async_copy(diag_v, diag_ref, out_s.at[1])
    diag_copy.start()
    wait_into(dsend, s_s.at[6])
    pltpu.make_async_copy(out_v, out_ref, out_s.at[0]).wait()
    diag_copy.wait()


def per_device(ancestor_inverse, factor_panel, pivot_inverse, sn_size, anc_list):
    rows, cols = factor_panel.shape
    kw = ancestor_inverse.shape[1]
    lrows = pivot_inverse.shape[0]
    vm, dma = pltpu.VMEM, pltpu.SemaphoreType.DMA
    bf, f32 = jnp.bfloat16, jnp.float32
    anys = pl.BlockSpec(memory_space=pl.ANY)
    return pl.pallas_call(
        kernel,
        out_shape=(jax.ShapeDtypeStruct((cols, rows), bf),
                   jax.ShapeDtypeStruct((lrows, cols), f32)),
        in_specs=[anys, anys, anys, pl.BlockSpec(memory_space=pltpu.SMEM), anys],
        out_specs=(anys, anys),
        scratch_shapes=[
            vm((4, rows, 2 * kw), bf),
            vm((rows, cols), bf),
            vm((lrows, cols), f32),
            vm(anc_list.shape, jnp.int32),
            vm((2, rows // 2, cols), bf),
            vm((2, 2, rows // 8, cols), bf),
            vm((4, 2 * kw, 4 * cols), bf),
            vm((2, rows // 2, W), bf),
            vm((16, cols), f32),
            vm((TOP * AB, 4 * cols), f32),
            vm((rows, cols), f32),
            vm((3, rows + 16 * MCH, cols), jnp.int16),
            vm((MCH, 4, 16 + TOP * AB, cols), jnp.int16),
            vm((MCH, TOP * AB, cols), f32),
            vm((TOP * AB, cols), f32),
            vm((TOP * AB, cols), bf),
            vm((W, cols), f32),
            vm((7, lrows + 16, cols), jnp.int16),
            vm((7, lrows + 16, cols), jnp.int16),
            vm((cols, rows), bf),
            vm((lrows, cols), f32),
            dma((4,)), dma((7,)), dma((2,)), dma((8,)), dma((8, 3)),
            dma((MCH, 2)), dma((MCH,)), dma((MCH, 4)), dma((3,)), dma((2,)),
        ],
        compiler_params=pltpu.CompilerParams(
            collective_id=0, has_side_effects=True, vmem_limit_bytes=60 * 1024 * 1024),
        cost_estimate=pl.CostEstimate(flops=5_000_000_000, bytes_accessed=4_000_000, transcendentals=0),
    )(ancestor_inverse, factor_panel, pivot_inverse, sn_size, anc_list)


def solution(mesh):
    return jax.shard_map(
        per_device,
        mesh=mesh,
        in_specs=(P("prow", "pcol"), P("prow", "pcol"), P("prow", "pcol"), P(), P()),
        out_specs=(P("pcol", "prow"), P("prow", "pcol")),
        check_vma=False,
    )
```

```python
import jax
import jax.numpy as jnp
from jax import lax
from jax.experimental import pallas as pl
from jax.experimental.pallas import tpu as pltpu
from jax.sharding import PartitionSpec as P

AB = 128
W = 512
MESH = pl.DeviceIdType.MESH
CHUNKS = (3, 3, 3, 2, 1)
MCH = len(CHUNKS)
TOP = max(CHUNKS)

FIRST = (
    ("spread_x", 0), ("relay_a", 0), ("own_send", 2), ("spread_x", 1), ("relay_x", 0), ("send_lead",), ("relay_a", 1),
    ("own_send", 3), ("own_send", 4), ("relay_x", 1), ("spread_x", 2), ("finish_a", 0), ("relay_a", 2),
)
REST = (
    ("wait_x", 0), ("wait_x", 1), ("spread_x", 3), ("wait_a", 0), ("compute", 0, 0, 2), ("relay_x", 2), ("finish_a", 1),
    ("wait_a", 1), ("compute", 1, 0, 2), ("merge", 0), ("relay_x", 3), ("relay_a", 3), ("relay_a", 4),
    ("wait_x", 2), ("compute", 0, 2, 3), ("finish_a", 2), ("merge", 1), ("fwd_lead",),
    ("wait_x", 3), ("wait_a", 2), ("compute", 2, 0, 4), ("finish_a", 3), ("finish_a", 4),
    ("wait_a", 3), ("compute", 3, 0, 4), ("merge", 2), ("wait_a", 4), ("compute", 4, 0, 4), ("compute", 1, 2, 4), ("compute", 0, 3, 4),
    ("wait_lead",), ("sent",), ("merge", 3), ("finish_c", 0), ("merge", 4),
    ("finish_c", 1), ("finish_c", 2), ("finish_c", 3), ("finish_c", 4),
)


def kernel(
    a_ref, l_ref, piv_ref, sn_ref, anc_ref, out_ref, diag_ref,
    abuf, l_in, piv, anc, lhat, away, lbuf, lead, live, acc, cown, csend, crecv, ckeep, tot, abf, corr, dsend, drecv, out_v, diag_v,
    in_sem, s_s, x_r, s2_r, s3_r, a_r, ab_r, c_r, h_r, out_s,
):
    rows = l_ref.shape[0]
    half = rows // 2
    quart = half // 4
    kw = a_ref.shape[1]
    first = [sum(CHUNKS[:m]) * AB for m in range(MCH)]
    p = lax.axis_index("prow")
    q = lax.axis_index("pcol")
    x, zh = p % 4, p // 4
    y, zl, c = q // 8, (q // 2) % 4, q % 2
    z = zh * 4 + zl
    k = q // 4

    def dev(x_, y_, z_, c_):
        return ((z_ // 4) * 4 + x_, y_ * 8 + (z_ % 4) * 2 + c_)

    other = ((zl + 2) % 4, 3 - zl, zl + 1 - 2 * (zl % 2), zl)

    def at_x(d):
        return dev((x + d) % 4, y, z, c)

    def at_y(d):
        return dev(x, (y + d) % 4, z, c)

    def at_z(z_):
        return dev(x, y, z_, c)

    sib = dev(x, y, z, 1 - c)

    def rcopy(src, dst, ssem, rsem, device):
        return pltpu.make_async_remote_copy(
            src_ref=src, dst_ref=dst, send_sem=ssem, recv_sem=rsem,
            device_id=device, device_id_type=MESH)

    barrier = pltpu.get_barrier_semaphore()
    partners = [at_z((z + d) % 8) for d in range(1, 8)]
    partners += [dev((x + d) % 4, y, ((zh + e) % 2) * 4 + zl, c)
                 for d in range(1, 4) for e in range(2)]
    partners += [at_y(1), at_y(3), sib]
    for partner in partners:
        pl.semaphore_signal(barrier, inc=1, device_id=partner, device_id_type=MESH)

    def mchunk(m):
        return pl.ds(first[m], CHUNKS[m] * AB)

    def mhalves(m):
        n = CHUNKS[m] * AB // 2
        return pl.ds(first[m], n), pl.ds(first[m] + n, n)

    def ablk(y_, c_, r):
        return abuf.at[y_, r, pl.ds(pl.multiple_of(c_ * kw, 128), kw)]

    a_load = pltpu.make_async_copy(a_ref, ablk(y, c, pl.ds(0, rows)), in_sem.at[3])
    l_load = pltpu.make_async_copy(l_ref, l_in, in_sem.at[0])
    anc_load = pltpu.make_async_copy(anc_ref, anc, in_sem.at[1])
    piv_load = pltpu.make_async_copy(piv_ref, piv, in_sem.at[2])
    l_load.start()
    anc_load.start()
    a_load.start()
    piv_load.start()

    l_load.wait()
    anc_load.wait()
    ids = p * (rows // AB) + lax.broadcasted_iota(jnp.int32, (16, anc_ref.shape[1]), 0)
    hit = jnp.where(ids == anc[pl.ds(k, 1), :], 1.0, 0.0)
    row_live = jnp.max(hit, axis=1, keepdims=True)
    cols = (q % 4) * AB + lax.broadcasted_iota(jnp.int32, (1, AB), 1)
    col_live = jnp.where(cols < sn_ref[k], 1.0, 0.0)
    live[...] = row_live * col_live
    for b in range(rows // AB):
        r = pl.ds(b * AB, AB)
        w = (l_in[r, :].astype(jnp.float32) * live[b:b + 1, :]).astype(jnp.bfloat16)
        lhat[b * AB // half, pl.ds(b * AB % half, AB), :] = w

    pl.semaphore_wait(barrier, len(partners))

    s1 = [rcopy(lhat.at[:, pl.ds((2 + i) * quart, quart), :], away.at[i], s_s.at[0], x_r.at[0], at_x(1 + 2 * i))
          for i in range(2)]
    for cp in s1:
        cp.start()

    def lanes(n):
        return pl.ds(n * AB, AB)

    def place(x_, zl_, zh_, i):
        home = 1 - (x_ + zl_ // 2) % 2
        xs = home * (x_ // 2) + (1 - home) * (((x_ + 3 + 2 * i) % 4) // 2)
        row = (1 - home) * 2 * quart + i * quart
        return zh_ * 2 + xs, pl.ds(pl.multiple_of(row, 64), quart)

    def s2(n, e, i, home):
        tz = other[n]
        src = lhat.at[tz % 2, pl.ds(i * quart, quart), :] if home else away.at[i, tz % 2]
        blk, row = place(x, tz, zh, i)
        dst = lbuf.at[blk, row, lanes(n)]
        sem = s2_r.at[2 * n + e]
        if n == 3 and e == 0:
            return pltpu.make_async_copy(src, dst, sem)
        return rcopy(src, dst, s_s.at[1], sem, at_z((zh + e) % 2 * 4 + tz))

    is_home = (x + zl // 2) % 2 == 0
    is_away = (x + zl // 2) % 2 == 1

    def s2_start(cond, home, *blocks):
        @pl.when(cond)
        def _():
            for n in blocks:
                for e in range(2):
                    for i in range(2):
                        s2(n, e, i, home).start()

    s2_start(is_away, True, 0, 1)
    s2_start(is_home, True, 2)

    zmate = z + 1 - 2 * (z % 2)

    def hblk(zb, cb):
        return lead.at[:, :, pl.ds(pl.multiple_of(((zb % 2) * 2 + cb) * AB, 128), AB)]

    h_own = [rcopy(lhat, hblk(z, c), s_s.at[4], h_r.at[0], at_z(zmate)),
             rcopy(lhat, hblk(z, c), s_s.at[4], h_r.at[1], sib)]
    h_fwd = rcopy(hblk(zmate, c), hblk(zmate, c), s_s.at[4], h_r.at[1], sib)
    h_loc = pltpu.make_async_copy(lhat, hblk(z, c), h_r.at[2])

    def send_lead():
        h_loc.start()
        for cp in h_own:
            cp.start()

    def a_own(m):
        r = mchunk(m)
        blk = ablk(y, c, r)
        return [rcopy(blk, blk, s_s.at[3], a_r.at[m, 0], at_y(1)),
                rcopy(blk, blk, s_s.at[3], a_r.at[m, 0], at_y(3)),
                rcopy(blk, blk, s_s.at[3], ab_r.at[m], sib)]

    ym, yp, yo = (y + 3) % 4, (y + 1) % 4, (y + 2) % 4

    def a_fwd(m):
        lo, hi = mhalves(m)
        r = mchunk(m)
        return [rcopy(ablk(ym, c, lo), ablk(ym, c, lo), s_s.at[3], a_r.at[m, 1], at_y(1)),
                rcopy(ablk(yp, c, hi), ablk(yp, c, hi), s_s.at[3], a_r.at[m, 1], at_y(3)),
                rcopy(ablk(ym, c, r), ablk(ym, c, r), s_s.at[3], ab_r.at[m], sib),
                rcopy(ablk(yp, c, r), ablk(yp, c, r), s_s.at[3], ab_r.at[m], sib)]

    def a_opp(m):
        r = mchunk(m)
        return [rcopy(ablk(yo, c, r), ablk(yo, c, r), s_s.at[3], ab_r.at[m], sib)]

    def wait_into(ref, sem):
        pltpu.make_async_copy(ref, ref, sem).wait()

    def own_send(m):
        for cp in a_own(m):
            cp.start()

    def relay_a(m):
        wait_into(abuf.at[pl.ds(0, 2), mchunk(m), pl.ds(0, kw)], a_r.at[m, 0])
        for cp in a_fwd(m):
            cp.start()

    def finish_a(m):
        wait_into(abuf.at[0, mchunk(m), pl.ds(0, kw)], a_r.at[m, 1])
        for cp in a_opp(m):
            cp.start()

    def wait_a(m):
        wait_into(abuf.at[:, mchunk(m), pl.ds(0, kw)], ab_r.at[m])

    a_load.wait()
    own_send(0)
    own_send(1)

    wait_into(away, x_r.at[0])
    s2_start(is_home, False, 0, 1)
    s2_start(is_home, True, 3)
    s2_start(is_away, False, 2, 3)

    def piece(n, e, x_, i):
        blk, row = place(x_, zl, (zh + e) % 2, i)
        return lbuf.at[blk, row, lanes(n)]

    xm, xp, xo = (x + 3) % 4, (x + 1) % 4, (x + 2) % 4

    def s3(n, e, i):
        k = 2 * n + e
        return [rcopy(piece(n, e, x, i), piece(n, e, x, i), s_s.at[2], s3_r.at[k, 0], at_x(1)),
                rcopy(piece(n, e, x, i), piece(n, e, x, i), s_s.at[2], s3_r.at[k, 1], at_x(3))]

    def s3_relay(n, e):
        k = 2 * n + e
        return [rcopy(piece(n, e, xm, 0), piece(n, e, xm, 0), s_s.at[2], s3_r.at[k, 2], at_x(1)),
                rcopy(piece(n, e, xp, 1), piece(n, e, xp, 1), s_s.at[2], s3_r.at[k, 2], at_x(3))]

    def wait_pair(sem):
        wait_into(lbuf.at[pl.ds(0, 2), pl.ds(0, quart), pl.ds(0, AB)], sem)

    def spread_x(n):
        for e in range(2):
            wait_pair(s2_r.at[2 * n + e])
            for i in range(2):
                for cp in s3(n, e, i):
                    cp.start()

    def relay_x(n):
        for e in range(2):
            cps = s3_relay(n, e)
            wait_pair(s3_r.at[2 * n + e, 0])
            cps[0].start()
            wait_pair(s3_r.at[2 * n + e, 1])
            cps[1].start()

    def wait_x(n):
        for e in range(2):
            wait_pair(s3_r.at[2 * n + e, 2])

    is_end = zl * (3 - zl) == 0
    def cout(m, n):
        return csend.at[n, pl.ds(first[m] + 16 * m, 16 + CHUNKS[m] * AB)]

    def c_copy(m, n, far=False):
        to, slot = (other[2], 3) if far else (other[n], n)
        t = pl.ds(0, 16 + CHUNKS[m] * AB)
        return rcopy(cout(m, n), crecv.at[m, slot, t], s_s.at[5], c_r.at[m, slot], at_z(zh * 4 + to))

    def code(part, dst, step=AB):
        n = part.shape[0]
        at = lax.broadcasted_iota(jnp.int32, (16, AB), 0)
        powers = jnp.zeros((16, AB), jnp.float32)
        for t in range(n // step):
            b = part[t * step:(t + 1) * step, :]
            top = jnp.max(jnp.abs(b), axis=0, keepdims=True)
            e = jnp.clip(jnp.floor(jnp.log2(jnp.maximum(top, 1e-30))) + 1.0, -90.0, 90.0)
            v = jnp.clip(jnp.round(b * jnp.exp2(15.0 - e)), -32767.0, 32767.0)
            dst[16 + t * step:16 + (t + 1) * step, :] = v.astype(jnp.int32).astype(jnp.int16)
            powers = jnp.where(at == t, e, powers)
        dst[0:16, :] = powers.astype(jnp.int32).astype(jnp.int16)

    def decode(src, t=0, step=AB):
        v = src[16 + t * step:16 + (t + 1) * step, :].astype(jnp.int32).astype(jnp.float32)
        e = src[0:16, :].astype(jnp.int32).astype(jnp.float32)
        return v * jnp.exp2(e[t:t + 1, :] - 15.0)

    is_inner = zl * (3 - zl) != 0

    def compute(m, n0, n1):
        r = mchunk(m)
        n = CHUNKS[m] * AB
        ln = pl.ds(n0 * AB, (n1 - n0) * AB)
        a = jnp.concatenate([abuf[yy, r, :] for yy in range(4)], axis=1)
        b = lbuf[:, :, ln].reshape(4 * lbuf.shape[1], (n1 - n0) * AB)
        acc[0:n, ln] = jnp.dot(a, b, preferred_element_type=jnp.float32)
        if n0 == 0:
            code(acc[0:n, AB:2 * AB], cout(m, 1))
            pl.when(is_end)(lambda: c_copy(m, 1, True).start())
            pl.when(is_inner)(lambda: c_copy(m, 1).start())
            ckeep[m, 0:n, :] = acc[0:n, 0:AB]

            @pl.when(is_end)
            def _():
                code(ckeep[m, 0:n, :], cout(m, 0))
                c_copy(m, 0).start()

        if n0 <= 2 < n1:
            code(acc[0:n, 2 * AB:3 * AB], cout(m, 2))
            c_copy(m, 2).start()
        if n1 == 4:
            cown[r, :] = acc[0:n, 3 * AB:4 * AB]

    def wait_c(m, slot):
        wait_into(crecv.at[m, slot, pl.ds(0, 16 + CHUNKS[m] * AB)], c_r.at[m, slot])

    def merge(m):
        @pl.when(is_inner)
        def _():
            wait_c(m, 3)
            for t in range(CHUNKS[m]):
                ckeep[m, t * AB:(t + 1) * AB, :] += decode(crecv.at[m, 3], t)
            code(ckeep[m, 0:CHUNKS[m] * AB, :], cout(m, 0))
            c_copy(m, 0).start()

    def add_slot(m, n):
        wait_c(m, n)
        for t in range(CHUNKS[m]):
            tot[t * AB:(t + 1) * AB, :] += decode(crecv.at[m, n], t)

    def out_copy(m):
        return pltpu.make_async_copy(out_v.at[:, mchunk(m)], out_ref.at[:, mchunk(m)], out_s.at[0])

    def finish_c(m):
        n = CHUNKS[m] * AB
        tot[0:n, :] = cown[mchunk(m), :]
        add_slot(m, 2)
        pl.when(is_inner)(lambda: add_slot(m, 1))
        add_slot(m, 0)
        for t in range(CHUNKS[m]):
            at = first[m] + t * AB
            b = at // AB
            v = -(tot[t * AB:(t + 1) * AB, :] * live[b:b + 1, :])
            abf[t * AB:(t + 1) * AB, :] = v.astype(jnp.bfloat16)
            out_v[:, at:at + AB] = v.T.astype(jnp.bfloat16)
        out_copy(m).start()
        part = lax.dot_general(
            lead[first[m] // half, pl.ds(first[m] % half, n), :], abf[0:n, :],
            (((0,), (0,)), ((), ())), preferred_element_type=jnp.float32)
        corr[...] = part if m == 0 else corr[...] + part

    def wait_lead():
        h_loc.wait()
        wait_into(lead.at[:, :, pl.ds(0, 2 * AB)], h_r.at[1])

    def fwd_lead():
        wait_into(hblk(zmate, c), h_r.at[0])
        h_fwd.start()

    def sent():
        wait_into(away, s_s.at[0])
        wait_into(abuf.at[0, pl.ds(0, 14 * quart * AB // (2 * kw)), :], s_s.at[1])
        wait_into(abuf.at[0], s_s.at[2])
        wait_into(abuf.at[:, pl.ds(0, rows * 7 // 8), :], s_s.at[3])
        wait_into(lead.at[:, :, pl.ds(0, 3 * AB)], s_s.at[4])

    steps = {f.__name__: f for f in (
        spread_x, relay_x, wait_x, own_send, relay_a, finish_a, wait_a, send_lead, fwd_lead, wait_lead,
        compute, merge, sent, finish_c)}

    def run(plan):
        for name, *at in plan:
            steps[name](*at)

    run(FIRST)
    run(REST)
    wait_into(csend, s_s.at[5])

    lrows = diag_ref.shape[0]

    def mine(p_):
        return pl.ds(pl.multiple_of(p_ * lrows, lrows), lrows)

    for d in (4, 1, 3, 2, 5, 7, 6):
        to = (zh + d // 4) % 2 * 4 + (x + d) % 4
        code(corr[mine(to), :], dsend.at[d - 1], lrows)
        cp = rcopy(dsend.at[d - 1], drecv.at[d - 1], s_s.at[6], x_r.at[1], (to, q))
        cp.start()
    total = corr[mine(p), :]
    wait_into(drecv, x_r.at[1])
    for d in range(1, 8):
        total = total + decode(drecv.at[d - 1], 0, lrows)
    lead_id = p * lrows + lax.broadcasted_iota(jnp.int32, (lrows, AB), 0)
    keep = jnp.where(lead_id < sn_ref[k], 1.0, 0.0) * col_live
    piv_load.wait()
    diag_v[...] = (piv[...] - total) * keep
    diag_copy = pltpu.make_async_copy(diag_v, diag_ref, out_s.at[1])
    diag_copy.start()
    wait_into(dsend, s_s.at[6])
    pltpu.make_async_copy(out_v, out_ref, out_s.at[0]).wait()
    diag_copy.wait()


def per_device(ancestor_inverse, factor_panel, pivot_inverse, sn_size, anc_list):
    rows, cols = factor_panel.shape
    kw = ancestor_inverse.shape[1]
    lrows = pivot_inverse.shape[0]
    vm, dma = pltpu.VMEM, pltpu.SemaphoreType.DMA
    bf, f32 = jnp.bfloat16, jnp.float32
    anys = pl.BlockSpec(memory_space=pl.ANY)
    return pl.pallas_call(
        kernel,
        out_shape=(jax.ShapeDtypeStruct((cols, rows), bf),
                   jax.ShapeDtypeStruct((lrows, cols), f32)),
        in_specs=[anys, anys, anys, pl.BlockSpec(memory_space=pltpu.SMEM), anys],
        out_specs=(anys, anys),
        scratch_shapes=[
            vm((4, rows, 2 * kw), bf),
            vm((rows, cols), bf),
            vm((lrows, cols), f32),
            vm(anc_list.shape, jnp.int32),
            vm((2, rows // 2, cols), bf),
            vm((2, 2, rows // 8, cols), bf),
            vm((4, 2 * kw, 4 * cols), bf),
            vm((2, rows // 2, W), bf),
            vm((16, cols), f32),
            vm((TOP * AB, 4 * cols), f32),
            vm((rows, cols), f32),
            vm((3, rows + 16 * MCH, cols), jnp.int16),
            vm((MCH, 4, 16 + TOP * AB, cols), jnp.int16),
            vm((MCH, TOP * AB, cols), f32),
            vm((TOP * AB, cols), f32),
            vm((TOP * AB, cols), bf),
            vm((W, cols), f32),
            vm((7, lrows + 16, cols), jnp.int16),
            vm((7, lrows + 16, cols), jnp.int16),
            vm((cols, rows), bf),
            vm((lrows, cols), f32),
            dma((4,)), dma((7,)), dma((2,)), dma((8,)), dma((8, 3)),
            dma((MCH, 2)), dma((MCH,)), dma((MCH, 4)), dma((3,)), dma((2,)),
        ],
        compiler_params=pltpu.CompilerParams(
            collective_id=0, has_side_effects=True, vmem_limit_bytes=60 * 1024 * 1024),
        cost_estimate=pl.CostEstimate(flops=5_000_000_000, bytes_accessed=4_000_000, transcendentals=0),
    )(ancestor_inverse, factor_panel, pivot_inverse, sn_size, anc_list)


def solution(mesh):
    return jax.shard_map(
        per_device,
        mesh=mesh,
        in_specs=(P("prow", "pcol"), P("prow", "pcol"), P("prow", "pcol"), P(), P()),
        out_specs=(P("pcol", "prow"), P("prow", "pcol")),
        check_vma=False,
    )
```

```python
import jax
import jax.numpy as jnp
from jax import lax
from jax.experimental import pallas as pl
from jax.experimental.pallas import tpu as pltpu
from jax.sharding import PartitionSpec as P

AB = 128
W = 512
MESH = pl.DeviceIdType.MESH
CHUNKS = (3, 3, 3, 3)
MCH = len(CHUNKS)
TOP = max(CHUNKS)

FIRST = (
    ("spread_x", 0), ("relay_a", 0), ("own_send", 2), ("spread_x", 1), ("relay_x", 0), ("send_lead",), ("relay_a", 1),
    ("own_send", 3), ("relay_x", 1), ("spread_x", 2), ("finish_a", 0), ("relay_a", 2),
)
REST = (
    ("wait_x", 0), ("wait_x", 1), ("spread_x", 3), ("wait_a", 0), ("compute", 0, 0, 2), ("finish_a", 1), ("relay_x", 2),
    ("wait_a", 1), ("compute", 1, 0, 2), ("merge", 0), ("relay_x", 3), ("relay_a", 3),
    ("wait_x", 2), ("compute", 0, 2, 3), ("finish_a", 2), ("merge", 1), ("fwd_lead",),
    ("wait_x", 3), ("wait_a", 2), ("compute", 2, 0, 4), ("finish_a", 3),
    ("wait_a", 3), ("compute", 3, 0, 4), ("merge", 2), ("compute", 1, 2, 4), ("compute", 0, 3, 4),
    ("wait_lead",), ("sent",), ("merge", 3), ("finish_c", 0),
    ("finish_c", 1), ("finish_c", 2), ("finish_c", 3),
)


def kernel(
    a_ref, l_ref, piv_ref, sn_ref, anc_ref, out_ref, diag_ref,
    abuf, l_in, piv, anc, lhat, away, lbuf, lead, live, acc, cown, csend, crecv, ckeep, tot, abf, corr, dsend, drecv, out_v, diag_v,
    in_sem, s_s, x_r, s2_r, s3_r, a_r, ab_r, c_r, h_r, out_s,
):
    rows = l_ref.shape[0]
    half = rows // 2
    quart = half // 4
    kw = a_ref.shape[1]
    first = [sum(CHUNKS[:m]) * AB for m in range(MCH)]
    p = lax.axis_index("prow")
    q = lax.axis_index("pcol")
    x, zh = p % 4, p // 4
    y, zl, c = q // 8, (q // 2) % 4, q % 2
    z = zh * 4 + zl
    k = q // 4

    def dev(x_, y_, z_, c_):
        return ((z_ // 4) * 4 + x_, y_ * 8 + (z_ % 4) * 2 + c_)

    other = ((zl + 2) % 4, 3 - zl, zl + 1 - 2 * (zl % 2), zl)

    def at_x(d):
        return dev((x + d) % 4, y, z, c)

    def at_y(d):
        return dev(x, (y + d) % 4, z, c)

    def at_z(z_):
        return dev(x, y, z_, c)

    sib = dev(x, y, z, 1 - c)

    def rcopy(src, dst, ssem, rsem, device):
        return pltpu.make_async_remote_copy(
            src_ref=src, dst_ref=dst, send_sem=ssem, recv_sem=rsem,
            device_id=device, device_id_type=MESH)

    def ablk(y_, c_, r):
        return abuf.at[y_, c_, r, :]

    a_load = pltpu.make_async_copy(a_ref, ablk(y, c, pl.ds(0, rows)), in_sem.at[3])
    l_load = pltpu.make_async_copy(l_ref, l_in, in_sem.at[0])
    anc_load = pltpu.make_async_copy(anc_ref, anc, in_sem.at[1])
    piv_load = pltpu.make_async_copy(piv_ref, piv, in_sem.at[2])
    l_load.start()
    anc_load.start()
    a_load.start()
    piv_load.start()

    barrier = pltpu.get_barrier_semaphore()
    partners = [at_z((z + d) % 8) for d in range(1, 8)]
    partners += [dev((x + d) % 4, y, ((zh + e) % 2) * 4 + zl, c)
                 for d in range(1, 4) for e in range(2)]
    partners += [at_y(1), at_y(3), sib]
    for partner in partners:
        pl.semaphore_signal(barrier, inc=1, device_id=partner, device_id_type=MESH)

    def mchunk(m):
        return pl.ds(first[m], CHUNKS[m] * AB)

    def mhalves(m):
        n = CHUNKS[m] * AB // 2
        return pl.ds(first[m], n), pl.ds(first[m] + n, n)

    l_load.wait()
    anc_load.wait()
    ids = p * (rows // AB) + lax.broadcasted_iota(jnp.int32, (16, anc_ref.shape[1]), 0)
    hit = jnp.where(ids == anc[pl.ds(k, 1), :], 1.0, 0.0)
    row_live = jnp.max(hit, axis=1, keepdims=True)
    cols = (q % 4) * AB + lax.broadcasted_iota(jnp.int32, (1, AB), 1)
    col_live = jnp.where(cols < sn_ref[k], 1.0, 0.0)
    live[...] = row_live * col_live
    for b in range(rows // AB):
        r = pl.ds(b * AB, AB)
        w = (l_in[r, :].astype(jnp.float32) * live[b:b + 1, :]).astype(jnp.bfloat16)
        lhat[b * AB // half, pl.ds(b * AB % half, AB), :] = w

    pl.semaphore_wait(barrier, len(partners))

    s1 = [rcopy(lhat.at[:, pl.ds((2 + i) * quart, quart), :], away.at[i], s_s.at[0], x_r.at[0], at_x(1 + 2 * i))
          for i in range(2)]
    for cp in s1:
        cp.start()

    def place(x_, zl_, zh_, i):
        home = 1 - (x_ + zl_ // 2) % 2
        xs = home * (x_ // 2) + (1 - home) * (((x_ + 3 + 2 * i) % 4) // 2)
        row = (1 - home) * 2 * quart + i * quart
        return zh_ * 2 + xs, pl.ds(pl.multiple_of(row, 64), quart)

    def s2(n, e, i, home):
        tz = other[n]
        src = lhat.at[tz % 2, pl.ds(i * quart, quart), :] if home else away.at[i, tz % 2]
        blk, row = place(x, tz, zh, i)
        dst = lbuf.at[n, blk, row]
        sem = s2_r.at[2 * n + e]
        if n == 3 and e == 0:
            return pltpu.make_async_copy(src, dst, sem)
        return rcopy(src, dst, s_s.at[1], sem, at_z((zh + e) % 2 * 4 + tz))

    is_home = (x + zl // 2) % 2 == 0
    is_away = (x + zl // 2) % 2 == 1

    def s2_start(cond, home, *blocks):
        @pl.when(cond)
        def _():
            for n in blocks:
                for e in range(2):
                    for i in range(2):
                        s2(n, e, i, home).start()

    s2_start(is_away, True, 0, 1)
    s2_start(is_home, True, 2)

    zmate = z + 1 - 2 * (z % 2)

    def hblk(zb, cb):
        return lead.at[(zb % 2) * 2 + cb]

    h_own = [rcopy(lhat, hblk(z, c), s_s.at[4], h_r.at[0], at_z(zmate)),
             rcopy(lhat, hblk(z, c), s_s.at[4], h_r.at[1], sib)]
    h_fwd = rcopy(hblk(zmate, c), hblk(zmate, c), s_s.at[4], h_r.at[1], sib)
    h_loc = pltpu.make_async_copy(lhat, hblk(z, c), h_r.at[2])

    def send_lead():
        h_loc.start()
        for cp in h_own:
            cp.start()

    def a_own(m):
        r = mchunk(m)
        blk = ablk(y, c, r)
        return [rcopy(blk, blk, s_s.at[3], a_r.at[m, 0], at_y(1)),
                rcopy(blk, blk, s_s.at[3], a_r.at[m, 0], at_y(3)),
                rcopy(blk, blk, s_s.at[3], ab_r.at[m], sib)]

    ym, yp, yo = (y + 3) % 4, (y + 1) % 4, (y + 2) % 4

    def a_fwd(m):
        lo, hi = mhalves(m)
        r = mchunk(m)
        return [rcopy(ablk(ym, c, lo), ablk(ym, c, lo), s_s.at[3], a_r.at[m, 1], at_y(1)),
                rcopy(ablk(yp, c, hi), ablk(yp, c, hi), s_s.at[3], a_r.at[m, 1], at_y(3)),
                rcopy(ablk(ym, c, r), ablk(ym, c, r), s_s.at[3], ab_r.at[m], sib),
                rcopy(ablk(yp, c, r), ablk(yp, c, r), s_s.at[3], ab_r.at[m], sib)]

    def a_opp(m):
        r = mchunk(m)
        return [rcopy(ablk(yo, c, r), ablk(yo, c, r), s_s.at[3], ab_r.at[m], sib)]

    def wait_into(ref, sem):
        pltpu.make_async_copy(ref, ref, sem).wait()

    def own_send(m):
        for cp in a_own(m):
            cp.start()

    def relay_a(m):
        wait_into(abuf.at[0, :, mchunk(m), :], a_r.at[m, 0])
        for cp in a_fwd(m):
            cp.start()

    def finish_a(m):
        wait_into(abuf.at[0, 0, mchunk(m), :], a_r.at[m, 1])
        for cp in a_opp(m):
            cp.start()

    def wait_a(m):
        wait_into(abuf.at[:, 0, mchunk(m), :], ab_r.at[m])

    a_load.wait()
    own_send(0)
    own_send(1)

    wait_into(away, x_r.at[0])
    s2_start(is_home, False, 0, 1)
    s2_start(is_home, True, 3)
    s2_start(is_away, False, 2, 3)

    def piece(n, e, x_, i):
        blk, row = place(x_, zl, (zh + e) % 2, i)
        return lbuf.at[n, blk, row]

    xm, xp, xo = (x + 3) % 4, (x + 1) % 4, (x + 2) % 4

    def s3(n, e, i):
        k = 2 * n + e
        return [rcopy(piece(n, e, x, i), piece(n, e, x, i), s_s.at[2], s3_r.at[k, 0], at_x(1)),
                rcopy(piece(n, e, x, i), piece(n, e, x, i), s_s.at[2], s3_r.at[k, 1], at_x(3))]

    def s3_relay(n, e):
        k = 2 * n + e
        return [rcopy(piece(n, e, xm, 0), piece(n, e, xm, 0), s_s.at[2], s3_r.at[k, 2], at_x(1)),
                rcopy(piece(n, e, xp, 1), piece(n, e, xp, 1), s_s.at[2], s3_r.at[k, 2], at_x(3))]

    def wait_pair(sem):
        wait_into(lbuf.at[0, pl.ds(0, 2), pl.ds(0, quart)], sem)

    def spread_x(n):
        for e in range(2):
            wait_pair(s2_r.at[2 * n + e])
            for i in range(2):
                for cp in s3(n, e, i):
                    cp.start()

    def relay_x(n):
        for e in range(2):
            cps = s3_relay(n, e)
            wait_pair(s3_r.at[2 * n + e, 0])
            cps[0].start()
            wait_pair(s3_r.at[2 * n + e, 1])
            cps[1].start()

    def wait_x(n):
        for e in range(2):
            wait_pair(s3_r.at[2 * n + e, 2])

    is_end = zl * (3 - zl) == 0
    def cout(m, n):
        return csend.at[n, pl.ds(first[m] + 16 * m, 16 + CHUNKS[m] * AB)]

    def c_copy(m, n, far=False):
        to, slot = (other[2], 3) if far else (other[n], n)
        t = pl.ds(0, 16 + CHUNKS[m] * AB)
        return rcopy(cout(m, n), crecv.at[m, slot, t], s_s.at[5], c_r.at[m, slot], at_z(zh * 4 + to))

    def code(part, dst, step=AB):
        n = part.shape[0]
        at = lax.broadcasted_iota(jnp.int32, (16, AB), 0)
        powers = jnp.zeros((16, AB), jnp.float32)
        for t in range(n // step):
            b = part[t * step:(t + 1) * step, :]
            top = jnp.max(jnp.abs(b), axis=0, keepdims=True)
            e = jnp.clip(jnp.floor(jnp.log2(jnp.maximum(top, 1e-30))) + 1.0, -90.0, 90.0)
            v = jnp.clip(jnp.round(b * jnp.exp2(15.0 - e)), -32767.0, 32767.0)
            dst[16 + t * step:16 + (t + 1) * step, :] = v.astype(jnp.int32).astype(jnp.int16)
            powers = jnp.where(at == t, e, powers)
        dst[0:16, :] = powers.astype(jnp.int32).astype(jnp.int16)

    def decode(src, t=0, step=AB):
        v = src[16 + t * step:16 + (t + 1) * step, :].astype(jnp.int32).astype(jnp.float32)
        e = src[0:16, :].astype(jnp.int32).astype(jnp.float32)
        return v * jnp.exp2(e[t:t + 1, :] - 15.0)

    is_inner = zl * (3 - zl) != 0

    def compute(m, n0, n1):
        r = mchunk(m)
        n = CHUNKS[m] * AB
        ln = pl.ds(n0 * AB, (n1 - n0) * AB)
        a = jnp.concatenate([abuf[yy, cc, r, :] for yy in range(4) for cc in range(2)], axis=1)
        b = jnp.concatenate([lbuf[j].reshape(8 * kw, AB) for j in range(n0, n1)], axis=1)
        acc[0:n, ln] = jnp.dot(a, b, preferred_element_type=jnp.float32)
        if n0 == 0:
            code(acc[0:n, AB:2 * AB], cout(m, 1))
            pl.when(is_end)(lambda: c_copy(m, 1, True).start())
            pl.when(is_inner)(lambda: c_copy(m, 1).start())
            ckeep[m, 0:n, :] = acc[0:n, 0:AB]

            @pl.when(is_end)
            def _():
                code(ckeep[m, 0:n, :], cout(m, 0))
                c_copy(m, 0).start()

        if n0 <= 2 < n1:
            code(acc[0:n, 2 * AB:3 * AB], cout(m, 2))
            c_copy(m, 2).start()
        if n1 == 4:
            cown[r, :] = acc[0:n, 3 * AB:4 * AB]

    def wait_c(m, slot):
        wait_into(crecv.at[m, slot, pl.ds(0, 16 + CHUNKS[m] * AB)], c_r.at[m, slot])

    def merge(m):
        @pl.when(is_inner)
        def _():
            wait_c(m, 3)
            for t in range(CHUNKS[m]):
                ckeep[m, t * AB:(t + 1) * AB, :] += decode(crecv.at[m, 3], t)
            code(ckeep[m, 0:CHUNKS[m] * AB, :], cout(m, 0))
            c_copy(m, 0).start()

    def add_slot(m, n):
        wait_c(m, n)
        for t in range(CHUNKS[m]):
            tot[t * AB:(t + 1) * AB, :] += decode(crecv.at[m, n], t)

    def out_copy(m):
        return pltpu.make_async_copy(out_v.at[:, mchunk(m)], out_ref.at[:, mchunk(m)], out_s.at[0])

    def finish_c(m):
        n = CHUNKS[m] * AB
        tot[0:n, :] = cown[mchunk(m), :]
        add_slot(m, 2)
        pl.when(is_inner)(lambda: add_slot(m, 1))
        add_slot(m, 0)
        for t in range(CHUNKS[m]):
            at = first[m] + t * AB
            b = at // AB
            v = -(tot[t * AB:(t + 1) * AB, :] * live[b:b + 1, :])
            abf[t * AB:(t + 1) * AB, :] = v.astype(jnp.bfloat16)
            out_v[:, at:at + AB] = v.T.astype(jnp.bfloat16)
        out_copy(m).start()
        lhs = jnp.concatenate([lead[j, first[m] // half, pl.ds(first[m] % half, n), :] for j in range(4)], axis=1)
        part = lax.dot_general(lhs, abf[0:n, :], (((0,), (0,)), ((), ())), preferred_element_type=jnp.float32)
        corr[...] = part if m == 0 else corr[...] + part

    def wait_lead():
        h_loc.wait()
        wait_into(lead.at[pl.ds(0, 2)], h_r.at[1])

    def fwd_lead():
        wait_into(hblk(zmate, c), h_r.at[0])
        h_fwd.start()

    def sent():
        wait_into(away, s_s.at[0])
        wait_into(abuf.at[0, 0, pl.ds(0, 14 * quart * AB // kw), :], s_s.at[1])
        wait_into(abuf.at[0], s_s.at[2])
        wait_into(abuf.at[:, :, pl.ds(0, rows * 7 // 8), :], s_s.at[3])
        wait_into(lead.at[pl.ds(0, 3)], s_s.at[4])

    steps = {f.__name__: f for f in (
        spread_x, relay_x, wait_x, own_send, relay_a, finish_a, wait_a, send_lead, fwd_lead, wait_lead,
        compute, merge, sent, finish_c)}

    def run(plan):
        for name, *at in plan:
            steps[name](*at)

    run(FIRST)
    run(REST)
    wait_into(csend, s_s.at[5])

    lrows = diag_ref.shape[0]

    def mine(p_):
        return pl.ds(pl.multiple_of(p_ * lrows, lrows), lrows)

    for d in (6, 5, 7, 4, 2, 1, 3):
        to = (zh + d // 4) % 2 * 4 + (x + d) % 4
        code(corr[mine(to), :], dsend.at[d - 1], lrows)
        cp = rcopy(dsend.at[d - 1], drecv.at[d - 1], s_s.at[6], x_r.at[1], (to, q))
        cp.start()
    total = corr[mine(p), :]
    wait_into(drecv, x_r.at[1])
    for d in range(1, 8):
        total = total + decode(drecv.at[d - 1], 0, lrows)
    lead_id = p * lrows + lax.broadcasted_iota(jnp.int32, (lrows, AB), 0)
    keep = jnp.where(lead_id < sn_ref[k], 1.0, 0.0) * col_live
    piv_load.wait()
    diag_v[...] = (piv[...] - total) * keep
    diag_copy = pltpu.make_async_copy(diag_v, diag_ref, out_s.at[1])
    diag_copy.start()
    wait_into(dsend, s_s.at[6])
    pltpu.make_async_copy(out_v, out_ref, out_s.at[0]).wait()
    diag_copy.wait()


def per_device(ancestor_inverse, factor_panel, pivot_inverse, sn_size, anc_list):
    rows, cols = factor_panel.shape
    kw = ancestor_inverse.shape[1]
    lrows = pivot_inverse.shape[0]
    vm, dma = pltpu.VMEM, pltpu.SemaphoreType.DMA
    bf, f32 = jnp.bfloat16, jnp.float32
    anys = pl.BlockSpec(memory_space=pl.ANY)
    return pl.pallas_call(
        kernel,
        out_shape=(jax.ShapeDtypeStruct((cols, rows), bf),
                   jax.ShapeDtypeStruct((lrows, cols), f32)),
        in_specs=[anys, anys, anys, pl.BlockSpec(memory_space=pltpu.SMEM), anys],
        out_specs=(anys, anys),
        scratch_shapes=[
            vm((4, 2, rows, kw), bf),
            vm((rows, cols), bf),
            vm((lrows, cols), f32),
            vm(anc_list.shape, jnp.int32),
            vm((2, rows // 2, cols), bf),
            vm((2, 2, rows // 8, cols), bf),
            vm((4, 4, 2 * kw, cols), bf),
            vm((4, 2, rows // 2, cols), bf),
            vm((16, cols), f32),
            vm((TOP * AB, 4 * cols), f32),
            vm((rows, cols), f32),
            vm((3, rows + 16 * MCH, cols), jnp.int16),
            vm((MCH, 4, 16 + TOP * AB, cols), jnp.int16),
            vm((MCH, TOP * AB, cols), f32),
            vm((TOP * AB, cols), f32),
            vm((TOP * AB, cols), bf),
            vm((W, cols), f32),
            vm((7, lrows + 16, cols), jnp.int16),
            vm((7, lrows + 16, cols), jnp.int16),
            vm((cols, rows), bf),
            vm((lrows, cols), f32),
            dma((4,)), dma((7,)), dma((2,)), dma((8,)), dma((8, 3)),
            dma((MCH, 2)), dma((MCH,)), dma((MCH, 4)), dma((3,)), dma((2,)),
        ],
        compiler_params=pltpu.CompilerParams(
            collective_id=0, has_side_effects=True, vmem_limit_bytes=60 * 1024 * 1024),
        cost_estimate=pl.CostEstimate(flops=5_000_000_000, bytes_accessed=4_000_000, transcendentals=0),
    )(ancestor_inverse, factor_panel, pivot_inverse, sn_size, anc_list)


def solution(mesh):
    return jax.shard_map(
        per_device,
        mesh=mesh,
        in_specs=(P("prow", "pcol"), P("prow", "pcol"), P("prow", "pcol"), P(), P()),
        out_specs=(P("pcol", "prow"), P("prow", "pcol")),
        check_vma=False,
    )
```

```python
import jax
import jax.numpy as jnp
from jax import lax
from jax.experimental import pallas as pl
from jax.experimental.pallas import tpu as pltpu
from jax.sharding import PartitionSpec as P

AB = 128
W = 512
MESH = pl.DeviceIdType.MESH
CHUNKS = (3, 3, 3, 3)
MCH = len(CHUNKS)
TOP = max(CHUNKS)

FIRST = (
    ("spread_x", 0), ("relay_a", 0), ("own_send", 2), ("spread_x", 1), ("relay_x", 0), ("send_lead",), ("relay_a", 1),
    ("own_send", 3), ("relay_x", 1), ("spread_x", 2), ("finish_a", 0), ("relay_a", 2),
)
REST = (
    ("wait_x", 0), ("wait_x", 1), ("spread_x", 3), ("wait_a", 0), ("compute", 0, 0, 2), ("finish_a", 1), ("relay_x", 2),
    ("wait_a", 1), ("compute", 1, 0, 2), ("merge", 0), ("relay_x", 3), ("relay_a", 3),
    ("wait_x", 2), ("compute", 0, 2, 3), ("finish_a", 2), ("merge", 1), ("fwd_lead",),
    ("wait_x", 3), ("wait_a", 2), ("compute", 2, 0, 4), ("finish_a", 3),
    ("wait_a", 3), ("compute", 3, 0, 4), ("merge", 2), ("compute", 1, 2, 4), ("compute", 0, 3, 4),
    ("wait_lead",), ("sent",), ("merge", 3), ("finish_c", 0),
    ("finish_c", 2), ("finish_c", 3), ("finish_c", 1),
)


def kernel(
    a_ref, l_ref, piv_ref, sn_ref, anc_ref, out_ref, diag_ref,
    abuf, l_in, piv, anc, lhat, away, lbuf, lead, live, acc, cown, csend, crecv, ckeep, abf, corr, dsend, drecv, out_v, diag_v,
    in_sem, s_s, x_r, s2_r, s3_r, a_r, ab_r, c_r, h_r, out_s,
):
    rows = l_ref.shape[0]
    half = rows // 2
    quart = half // 4
    kw = a_ref.shape[1]
    first = [sum(CHUNKS[:m]) * AB for m in range(MCH)]
    p = lax.axis_index("prow")
    q = lax.axis_index("pcol")
    x, zh = p % 4, p // 4
    y, zl, c = q // 8, (q // 2) % 4, q % 2
    z = zh * 4 + zl
    k = q // 4

    def dev(x_, y_, z_, c_):
        return ((z_ // 4) * 4 + x_, y_ * 8 + (z_ % 4) * 2 + c_)

    other = ((zl + 2) % 4, 3 - zl, zl + 1 - 2 * (zl % 2), zl)

    def at_x(d):
        return dev((x + d) % 4, y, z, c)

    def at_y(d):
        return dev(x, (y + d) % 4, z, c)

    def at_z(z_):
        return dev(x, y, z_, c)

    sib = dev(x, y, z, 1 - c)

    def rcopy(src, dst, ssem, rsem, device):
        return pltpu.make_async_remote_copy(
            src_ref=src, dst_ref=dst, send_sem=ssem, recv_sem=rsem,
            device_id=device, device_id_type=MESH)

    def ablk(y_, c_, r):
        return abuf.at[y_, c_, r, :]

    a_load = pltpu.make_async_copy(a_ref, ablk(y, c, pl.ds(0, rows)), in_sem.at[3])
    l_load = pltpu.make_async_copy(l_ref, l_in, in_sem.at[0])
    anc_load = pltpu.make_async_copy(anc_ref, anc, in_sem.at[1])
    piv_load = pltpu.make_async_copy(piv_ref, piv, in_sem.at[2])
    l_load.start()
    anc_load.start()
    a_load.start()
    piv_load.start()

    barrier = pltpu.get_barrier_semaphore()
    partners = [at_z((z + d) % 8) for d in range(1, 8)]
    partners += [dev((x + d) % 4, y, ((zh + e) % 2) * 4 + zl, c)
                 for d in range(1, 4) for e in range(2)]
    partners += [at_y(1), at_y(3), sib]
    for partner in partners:
        pl.semaphore_signal(barrier, inc=1, device_id=partner, device_id_type=MESH)

    def mchunk(m):
        return pl.ds(first[m], CHUNKS[m] * AB)

    def mhalves(m):
        n = CHUNKS[m] * AB // 2
        return pl.ds(first[m], n), pl.ds(first[m] + n, n)

    l_load.wait()
    anc_load.wait()
    ids = p * (rows // AB) + lax.broadcasted_iota(jnp.int32, (16, anc_ref.shape[1]), 0)
    hit = jnp.where(ids == anc[pl.ds(k, 1), :], 1.0, 0.0)
    row_live = jnp.max(hit, axis=1, keepdims=True)
    cols = (q % 4) * AB + lax.broadcasted_iota(jnp.int32, (1, AB), 1)
    col_live = jnp.where(cols < sn_ref[k], 1.0, 0.0)
    live[...] = row_live * col_live
    for b in range(rows // AB):
        r = pl.ds(b * AB, AB)
        w = (l_in[r, :].astype(jnp.float32) * live[b:b + 1, :]).astype(jnp.bfloat16)
        lhat[b * AB // half, pl.ds(b * AB % half, AB), :] = w

    pl.semaphore_wait(barrier, len(partners))

    s1 = [rcopy(lhat.at[:, pl.ds((2 + i) * quart, quart), :], away.at[i], s_s.at[0], x_r.at[0], at_x(1 + 2 * i))
          for i in range(2)]
    for cp in s1:
        cp.start()

    def place(x_, zl_, zh_, i):
        home = 1 - (x_ + zl_ // 2) % 2
        xs = home * (x_ // 2) + (1 - home) * (((x_ + 3 + 2 * i) % 4) // 2)
        row = (1 - home) * 2 * quart + i * quart
        return zh_ * 2 + xs, pl.ds(pl.multiple_of(row, 64), quart)

    def s2(n, e, i, home):
        tz = other[n]
        src = lhat.at[tz % 2, pl.ds(i * quart, quart), :] if home else away.at[i, tz % 2]
        blk, row = place(x, tz, zh, i)
        dst = lbuf.at[n, blk, row]
        sem = s2_r.at[2 * n + e]
        if n == 3 and e == 0:
            return pltpu.make_async_copy(src, dst, sem)
        return rcopy(src, dst, s_s.at[1], sem, at_z((zh + e) % 2 * 4 + tz))

    is_home = (x + zl // 2) % 2 == 0
    is_away = (x + zl // 2) % 2 == 1

    def s2_start(cond, home, *blocks):
        @pl.when(cond)
        def _():
            for n in blocks:
                for e in range(2):
                    for i in range(2):
                        s2(n, e, i, home).start()

    s2_start(is_away, True, 0, 1)
    s2_start(is_home, True, 2)

    zmate = z + 1 - 2 * (z % 2)

    def hblk(zb, cb):
        return lead.at[(zb % 2) * 2 + cb]

    h_own = [rcopy(lhat, hblk(z, c), s_s.at[4], h_r.at[0], at_z(zmate)),
             rcopy(lhat, hblk(z, c), s_s.at[4], h_r.at[1], sib)]
    h_fwd = rcopy(hblk(zmate, c), hblk(zmate, c), s_s.at[4], h_r.at[1], sib)
    h_loc = pltpu.make_async_copy(lhat, hblk(z, c), h_r.at[2])

    def send_lead():
        h_loc.start()
        for cp in h_own:
            cp.start()

    def a_own(m):
        r = mchunk(m)
        blk = ablk(y, c, r)
        return [rcopy(blk, blk, s_s.at[3], a_r.at[m, 0], at_y(1)),
                rcopy(blk, blk, s_s.at[3], a_r.at[m, 0], at_y(3)),
                rcopy(blk, blk, s_s.at[3], ab_r.at[m], sib)]

    ym, yp, yo = (y + 3) % 4, (y + 1) % 4, (y + 2) % 4

    def a_fwd(m):
        lo, hi = mhalves(m)
        r = mchunk(m)
        return [rcopy(ablk(ym, c, lo), ablk(ym, c, lo), s_s.at[3], a_r.at[m, 1], at_y(1)),
                rcopy(ablk(yp, c, hi), ablk(yp, c, hi), s_s.at[3], a_r.at[m, 1], at_y(3)),
                rcopy(ablk(ym, c, r), ablk(ym, c, r), s_s.at[3], ab_r.at[m], sib),
                rcopy(ablk(yp, c, r), ablk(yp, c, r), s_s.at[3], ab_r.at[m], sib)]

    def a_opp(m):
        r = mchunk(m)
        return [rcopy(ablk(yo, c, r), ablk(yo, c, r), s_s.at[3], ab_r.at[m], sib)]

    def wait_into(ref, sem):
        pltpu.make_async_copy(ref, ref, sem).wait()

    def own_send(m):
        for cp in a_own(m):
            cp.start()

    def relay_a(m):
        wait_into(abuf.at[0, :, mchunk(m), :], a_r.at[m, 0])
        for cp in a_fwd(m):
            cp.start()

    def finish_a(m):
        wait_into(abuf.at[0, 0, mchunk(m), :], a_r.at[m, 1])
        for cp in a_opp(m):
            cp.start()

    def wait_a(m):
        wait_into(abuf.at[:, 0, mchunk(m), :], ab_r.at[m])

    a_load.wait()
    own_send(0)
    own_send(1)

    wait_into(away, x_r.at[0])
    s2_start(is_home, False, 0, 1)
    s2_start(is_home, True, 3)
    s2_start(is_away, False, 2, 3)

    def piece(n, e, x_, i):
        blk, row = place(x_, zl, (zh + e) % 2, i)
        return lbuf.at[n, blk, row]

    xm, xp, xo = (x + 3) % 4, (x + 1) % 4, (x + 2) % 4

    def s3(n, e, i):
        k = 2 * n + e
        return [rcopy(piece(n, e, x, i), piece(n, e, x, i), s_s.at[2], s3_r.at[k, 0], at_x(1)),
                rcopy(piece(n, e, x, i), piece(n, e, x, i), s_s.at[2], s3_r.at[k, 1], at_x(3))]

    def s3_relay(n, e):
        k = 2 * n + e
        return [rcopy(piece(n, e, xm, 0), piece(n, e, xm, 0), s_s.at[2], s3_r.at[k, 2], at_x(1)),
                rcopy(piece(n, e, xp, 1), piece(n, e, xp, 1), s_s.at[2], s3_r.at[k, 2], at_x(3))]

    def wait_pair(sem):
        wait_into(lbuf.at[0, pl.ds(0, 2), pl.ds(0, quart)], sem)

    def spread_x(n):
        for e in range(2):
            wait_pair(s2_r.at[2 * n + e])
            for i in range(2):
                for cp in s3(n, e, i):
                    cp.start()

    def relay_x(n):
        for e in range(2):
            cps = s3_relay(n, e)
            wait_pair(s3_r.at[2 * n + e, 0])
            cps[0].start()
            wait_pair(s3_r.at[2 * n + e, 1])
            cps[1].start()

    def wait_x(n):
        for e in range(2):
            wait_pair(s3_r.at[2 * n + e, 2])

    is_end = zl * (3 - zl) == 0
    def cout(m, n):
        return csend.at[n, pl.ds(first[m] + 16 * m, 16 + CHUNKS[m] * AB)]

    def c_copy(m, n, far=False):
        to, slot = (other[2], 3) if far else (other[n], n)
        t = pl.ds(0, 16 + CHUNKS[m] * AB)
        return rcopy(cout(m, n), crecv.at[m, slot, t], s_s.at[5], c_r.at[m, slot], at_z(zh * 4 + to))

    def code(part, dst, step=AB):
        n = part.shape[0]
        at = lax.broadcasted_iota(jnp.int32, (16, AB), 0)
        powers = jnp.zeros((16, AB), jnp.float32)
        for t in range(n // step):
            b = part[t * step:(t + 1) * step, :]
            top = jnp.max(jnp.abs(b), axis=0, keepdims=True)
            e = jnp.clip(jnp.floor(jnp.log2(jnp.maximum(top, 1e-30))) + 1.0, -90.0, 90.0)
            v = jnp.clip(jnp.round(b * jnp.exp2(15.0 - e)), -32767.0, 32767.0)
            dst[16 + t * step:16 + (t + 1) * step, :] = v.astype(jnp.int32).astype(jnp.int16)
            powers = jnp.where(at == t, e, powers)
        dst[0:16, :] = powers.astype(jnp.int32).astype(jnp.int16)

    def decode(src, t=0, step=AB):
        v = src[16 + t * step:16 + (t + 1) * step, :].astype(jnp.int32).astype(jnp.float32)
        e = src[0:16, :].astype(jnp.int32).astype(jnp.float32)
        return v * jnp.exp2(e[t:t + 1, :] - 15.0)

    is_inner = zl * (3 - zl) != 0

    def compute(m, n0, n1):
        r = mchunk(m)
        n = CHUNKS[m] * AB
        ln = pl.ds(n0 * AB, (n1 - n0) * AB)
        a = jnp.concatenate([abuf[yy, cc, r, :] for yy in range(4) for cc in range(2)], axis=1)
        b = jnp.concatenate([lbuf[j].reshape(8 * kw, AB) for j in range(n0, n1)], axis=1)
        acc[0:n, ln] = jnp.dot(a, b, preferred_element_type=jnp.float32)
        if n0 == 0:
            code(acc[0:n, AB:2 * AB], cout(m, 1))
            pl.when(is_end)(lambda: c_copy(m, 1, True).start())
            pl.when(is_inner)(lambda: c_copy(m, 1).start())
            ckeep[m, 0:n, :] = acc[0:n, 0:AB]

            @pl.when(is_end)
            def _():
                code(ckeep[m, 0:n, :], cout(m, 0))
                c_copy(m, 0).start()

        if n0 <= 2 < n1:
            code(acc[0:n, 2 * AB:3 * AB], cout(m, 2))
            c_copy(m, 2).start()
        if n1 == 4:
            cown[r, :] = acc[0:n, 3 * AB:4 * AB]

    def wait_c(m, slot):
        wait_into(crecv.at[m, slot, pl.ds(0, 16 + CHUNKS[m] * AB)], c_r.at[m, slot])

    def merge(m):
        @pl.when(is_inner)
        def _():
            wait_c(m, 3)
            for t in range(CHUNKS[m]):
                ckeep[m, t * AB:(t + 1) * AB, :] += decode(crecv.at[m, 3], t)
            code(ckeep[m, 0:CHUNKS[m] * AB, :], cout(m, 0))
            c_copy(m, 0).start()

    def add_slot(m, n):
        wait_c(m, n)
        for t in range(CHUNKS[m]):
            cown[first[m] + t * AB:first[m] + (t + 1) * AB, :] += decode(crecv.at[m, n], t)

    def out_copy(m):
        return pltpu.make_async_copy(out_v.at[:, mchunk(m)], out_ref.at[:, mchunk(m)], out_s.at[0])

    def value(m, t):
        at = first[m] + t * AB
        return -(cown[at:at + AB, :] * live[at // AB:at // AB + 1, :])

    def store_out(m):
        for t in range(CHUNKS[m]):
            at = first[m] + t * AB
            out_v[:, at:at + AB] = value(m, t).T.astype(jnp.bfloat16)
        out_copy(m).start()

    def finish_c(m):
        n = CHUNKS[m] * AB
        add_slot(m, 2)
        pl.when(is_inner)(lambda: add_slot(m, 1))
        add_slot(m, 0)
        for t in range(CHUNKS[m]):
            abf[t * AB:(t + 1) * AB, :] = value(m, t).astype(jnp.bfloat16)
        lhs = jnp.concatenate([lead[j, first[m] // half, pl.ds(first[m] % half, n), :] for j in range(4)], axis=1)
        part = lax.dot_general(lhs, abf[0:n, :], (((0,), (0,)), ((), ())), preferred_element_type=jnp.float32)
        corr[...] = part if m == 0 else corr[...] + part

    def wait_lead():
        h_loc.wait()
        wait_into(lead.at[pl.ds(0, 2)], h_r.at[1])

    def fwd_lead():
        wait_into(hblk(zmate, c), h_r.at[0])
        h_fwd.start()

    def sent():
        wait_into(away, s_s.at[0])
        wait_into(abuf.at[0, 0, pl.ds(0, 14 * quart * AB // kw), :], s_s.at[1])
        wait_into(abuf.at[0], s_s.at[2])
        wait_into(abuf.at[:, :, pl.ds(0, rows * 7 // 8), :], s_s.at[3])
        wait_into(lead.at[pl.ds(0, 3)], s_s.at[4])

    steps = {f.__name__: f for f in (
        spread_x, relay_x, wait_x, own_send, relay_a, finish_a, wait_a, send_lead, fwd_lead, wait_lead,
        compute, merge, sent, finish_c)}

    def run(plan):
        for name, *at in plan:
            steps[name](*at)

    run(FIRST)
    run(REST)
    wait_into(csend, s_s.at[5])

    lrows = diag_ref.shape[0]

    def mine(p_):
        return pl.ds(pl.multiple_of(p_ * lrows, lrows), lrows)

    for d in (6, 5, 7, 4, 2, 1, 3):
        to = (zh + d // 4) % 2 * 4 + (x + d) % 4
        code(corr[mine(to), :], dsend.at[d - 1], lrows)
        cp = rcopy(dsend.at[d - 1], drecv.at[d - 1], s_s.at[6], x_r.at[1], (to, q))
        cp.start()
    for m in range(MCH):
        store_out(m)
    total = corr[mine(p), :]
    wait_into(drecv, x_r.at[1])
    for d in range(1, 8):
        total = total + decode(drecv.at[d - 1], 0, lrows)
    lead_id = p * lrows + lax.broadcasted_iota(jnp.int32, (lrows, AB), 0)
    keep = jnp.where(lead_id < sn_ref[k], 1.0, 0.0) * col_live
    piv_load.wait()
    diag_v[...] = (piv[...] - total) * keep
    diag_copy = pltpu.make_async_copy(diag_v, diag_ref, out_s.at[1])
    diag_copy.start()
    wait_into(dsend, s_s.at[6])
    pltpu.make_async_copy(out_v, out_ref, out_s.at[0]).wait()
    diag_copy.wait()


def per_device(ancestor_inverse, factor_panel, pivot_inverse, sn_size, anc_list):
    rows, cols = factor_panel.shape
    kw = ancestor_inverse.shape[1]
    lrows = pivot_inverse.shape[0]
    vm, dma = pltpu.VMEM, pltpu.SemaphoreType.DMA
    bf, f32 = jnp.bfloat16, jnp.float32
    anys = pl.BlockSpec(memory_space=pl.ANY)
    return pl.pallas_call(
        kernel,
        out_shape=(jax.ShapeDtypeStruct((cols, rows), bf),
                   jax.ShapeDtypeStruct((lrows, cols), f32)),
        in_specs=[anys, anys, anys, pl.BlockSpec(memory_space=pltpu.SMEM), anys],
        out_specs=(anys, anys),
        scratch_shapes=[
            vm((4, 2, rows, kw), bf),
            vm((rows, cols), bf),
            vm((lrows, cols), f32),
            vm(anc_list.shape, jnp.int32),
            vm((2, rows // 2, cols), bf),
            vm((2, 2, rows // 8, cols), bf),
            vm((4, 4, 2 * kw, cols), bf),
            vm((4, 2, rows // 2, cols), bf),
            vm((16, cols), f32),
            vm((TOP * AB, 4 * cols), f32),
            vm((rows, cols), f32),
            vm((3, rows + 16 * MCH, cols), jnp.int16),
            vm((MCH, 4, 16 + TOP * AB, cols), jnp.int16),
            vm((MCH, TOP * AB, cols), f32),
            vm((TOP * AB, cols), bf),
            vm((W, cols), f32),
            vm((7, lrows + 16, cols), jnp.int16),
            vm((7, lrows + 16, cols), jnp.int16),
            vm((cols, rows), bf),
            vm((lrows, cols), f32),
            dma((4,)), dma((7,)), dma((2,)), dma((8,)), dma((8, 3)),
            dma((MCH, 2)), dma((MCH,)), dma((MCH, 4)), dma((3,)), dma((2,)),
        ],
        compiler_params=pltpu.CompilerParams(
            collective_id=0, has_side_effects=True, vmem_limit_bytes=60 * 1024 * 1024),
        cost_estimate=pl.CostEstimate(flops=5_000_000_000, bytes_accessed=4_000_000, transcendentals=0),
    )(ancestor_inverse, factor_panel, pivot_inverse, sn_size, anc_list)


def solution(mesh):
    return jax.shard_map(
        per_device,
        mesh=mesh,
        in_specs=(P("prow", "pcol"), P("prow", "pcol"), P("prow", "pcol"), P(), P()),
        out_specs=(P("pcol", "prow"), P("prow", "pcol")),
        check_vma=False,
    )
```

```python
import jax
import jax.numpy as jnp
from jax import lax
from jax.experimental import pallas as pl
from jax.experimental.pallas import tpu as pltpu
from jax.sharding import PartitionSpec as P

AB = 128
W = 512
MESH = pl.DeviceIdType.MESH
CHUNKS = (3, 3, 3, 3)
MCH = len(CHUNKS)
TOP = max(CHUNKS)

FIRST = (
    ("spread_x", 0), ("relay_a", 0), ("own_send", 2), ("spread_x", 1), ("relay_x", 0), ("send_lead",), ("relay_a", 1),
    ("own_send", 3), ("relay_x", 1), ("spread_x", 2), ("finish_a", 0), ("relay_a", 2),
)
REST = (
    ("wait_x", 0), ("wait_x", 1), ("spread_x", 3), ("wait_a", 0), ("compute", 0, 0, 2), ("finish_a", 1), ("relay_x", 2),
    ("wait_a", 1), ("compute", 1, 0, 2), ("merge", 0), ("relay_x", 3), ("relay_a", 3),
    ("wait_x", 2), ("compute", 0, 2, 3), ("finish_a", 2), ("merge", 1), ("fwd_lead",),
    ("wait_x", 3), ("wait_a", 2), ("compute", 2, 0, 4), ("finish_a", 3),
    ("wait_a", 3), ("compute", 3, 0, 4), ("merge", 2), ("compute", 1, 2, 4), ("compute", 0, 3, 4),
    ("wait_lead",), ("sent",), ("merge", 3), ("finish_c", 0),
)
INNER = (("finish_c", 2), ("finish_c", 3), ("finish_c", 1))
END = (("finish_c", 1), ("finish_c", 2), ("finish_c", 3))


def kernel(
    a_ref, l_ref, piv_ref, sn_ref, anc_ref, out_ref, diag_ref,
    abuf, l_in, piv, anc, lhat, away, lbuf, lead, live, acc, cown, csend, crecv, ckeep, abf, corr, dsend, drecv, out_v, diag_v,
    in_sem, s_s, x_r, s2_r, s3_r, a_r, ab_r, c_r, h_r, out_s,
):
    rows = l_ref.shape[0]
    half = rows // 2
    quart = half // 4
    kw = a_ref.shape[1]
    first = [sum(CHUNKS[:m]) * AB for m in range(MCH)]
    p = lax.axis_index("prow")
    q = lax.axis_index("pcol")
    x, zh = p % 4, p // 4
    y, zl, c = q // 8, (q // 2) % 4, q % 2
    z = zh * 4 + zl
    k = q // 4

    def dev(x_, y_, z_, c_):
        return ((z_ // 4) * 4 + x_, y_ * 8 + (z_ % 4) * 2 + c_)

    other = ((zl + 2) % 4, 3 - zl, zl + 1 - 2 * (zl % 2), zl)

    def at_x(d):
        return dev((x + d) % 4, y, z, c)

    def at_y(d):
        return dev(x, (y + d) % 4, z, c)

    def at_z(z_):
        return dev(x, y, z_, c)

    sib = dev(x, y, z, 1 - c)

    def rcopy(src, dst, ssem, rsem, device):
        return pltpu.make_async_remote_copy(
            src_ref=src, dst_ref=dst, send_sem=ssem, recv_sem=rsem,
            device_id=device, device_id_type=MESH)

    def ablk(y_, c_, r):
        return abuf.at[y_, c_, r, :]

    a_load = pltpu.make_async_copy(a_ref, ablk(y, c, pl.ds(0, rows)), in_sem.at[3])
    l_load = pltpu.make_async_copy(l_ref, l_in, in_sem.at[0])
    anc_load = pltpu.make_async_copy(anc_ref, anc, in_sem.at[1])
    piv_load = pltpu.make_async_copy(piv_ref, piv, in_sem.at[2])
    l_load.start()
    anc_load.start()
    a_load.start()
    piv_load.start()

    barrier = pltpu.get_barrier_semaphore()
    partners = [at_z((z + d) % 8) for d in range(1, 8)]
    partners += [dev((x + d) % 4, y, ((zh + e) % 2) * 4 + zl, c)
                 for d in range(1, 4) for e in range(2)]
    partners += [at_y(1), at_y(3), sib]
    for partner in partners:
        pl.semaphore_signal(barrier, inc=1, device_id=partner, device_id_type=MESH)

    def mchunk(m):
        return pl.ds(first[m], CHUNKS[m] * AB)

    def mhalves(m):
        n = CHUNKS[m] * AB // 2
        return pl.ds(first[m], n), pl.ds(first[m] + n, n)

    l_load.wait()
    anc_load.wait()
    ids = p * (rows // AB) + lax.broadcasted_iota(jnp.int32, (16, anc_ref.shape[1]), 0)
    hit = jnp.where(ids == anc[pl.ds(k, 1), :], 1.0, 0.0)
    row_live = jnp.max(hit, axis=1, keepdims=True)
    cols = (q % 4) * AB + lax.broadcasted_iota(jnp.int32, (1, AB), 1)
    col_live = jnp.where(cols < sn_ref[k], 1.0, 0.0)
    live[...] = row_live * col_live
    for b in range(rows // AB):
        r = pl.ds(b * AB, AB)
        w = (l_in[r, :].astype(jnp.float32) * live[b:b + 1, :]).astype(jnp.bfloat16)
        lhat[b * AB // half, pl.ds(b * AB % half, AB), :] = w

    pl.semaphore_wait(barrier, len(partners))

    s1 = [rcopy(lhat.at[:, pl.ds((2 + i) * quart, quart), :], away.at[i], s_s.at[0], x_r.at[0], at_x(1 + 2 * i))
          for i in range(2)]
    for cp in s1:
        cp.start()

    def place(x_, zl_, zh_, i):
        home = 1 - (x_ + zl_ // 2) % 2
        xs = home * (x_ // 2) + (1 - home) * (((x_ + 3 + 2 * i) % 4) // 2)
        row = (1 - home) * 2 * quart + i * quart
        return zh_ * 2 + xs, pl.ds(pl.multiple_of(row, 64), quart)

    def s2(n, e, i, home):
        tz = other[n]
        src = lhat.at[tz % 2, pl.ds(i * quart, quart), :] if home else away.at[i, tz % 2]
        blk, row = place(x, tz, zh, i)
        dst = lbuf.at[n, blk, row]
        sem = s2_r.at[2 * n + e]
        if n == 3 and e == 0:
            return pltpu.make_async_copy(src, dst, sem)
        return rcopy(src, dst, s_s.at[1], sem, at_z((zh + e) % 2 * 4 + tz))

    is_home = (x + zl // 2) % 2 == 0
    is_away = (x + zl // 2) % 2 == 1

    def s2_start(cond, home, *blocks):
        @pl.when(cond)
        def _():
            for n in blocks:
                for e in range(2):
                    for i in range(2):
                        s2(n, e, i, home).start()

    s2_start(is_away, True, 0, 1)
    s2_start(is_home, True, 2)

    zmate = z + 1 - 2 * (z % 2)

    def hblk(zb, cb):
        return lead.at[(zb % 2) * 2 + cb]

    h_own = [rcopy(lhat, hblk(z, c), s_s.at[4], h_r.at[0], at_z(zmate)),
             rcopy(lhat, hblk(z, c), s_s.at[4], h_r.at[1], sib)]
    h_fwd = rcopy(hblk(zmate, c), hblk(zmate, c), s_s.at[4], h_r.at[1], sib)
    h_loc = pltpu.make_async_copy(lhat, hblk(z, c), h_r.at[2])

    def send_lead():
        h_loc.start()
        for cp in h_own:
            cp.start()

    def a_own(m):
        r = mchunk(m)
        blk = ablk(y, c, r)
        return [rcopy(blk, blk, s_s.at[3], a_r.at[m, 0], at_y(1)),
                rcopy(blk, blk, s_s.at[3], a_r.at[m, 0], at_y(3)),
                rcopy(blk, blk, s_s.at[3], ab_r.at[m], sib)]

    ym, yp, yo = (y + 3) % 4, (y + 1) % 4, (y + 2) % 4

    def a_fwd(m):
        lo, hi = mhalves(m)
        r = mchunk(m)
        return [rcopy(ablk(ym, c, lo), ablk(ym, c, lo), s_s.at[3], a_r.at[m, 1], at_y(1)),
                rcopy(ablk(yp, c, hi), ablk(yp, c, hi), s_s.at[3], a_r.at[m, 1], at_y(3)),
                rcopy(ablk(ym, c, r), ablk(ym, c, r), s_s.at[3], ab_r.at[m], sib),
                rcopy(ablk(yp, c, r), ablk(yp, c, r), s_s.at[3], ab_r.at[m], sib)]

    def a_opp(m):
        r = mchunk(m)
        return [rcopy(ablk(yo, c, r), ablk(yo, c, r), s_s.at[3], ab_r.at[m], sib)]

    def wait_into(ref, sem):
        pltpu.make_async_copy(ref, ref, sem).wait()

    def own_send(m):
        for cp in a_own(m):
            cp.start()

    def relay_a(m):
        wait_into(abuf.at[0, :, mchunk(m), :], a_r.at[m, 0])
        for cp in a_fwd(m):
            cp.start()

    def finish_a(m):
        wait_into(abuf.at[0, 0, mchunk(m), :], a_r.at[m, 1])
        for cp in a_opp(m):
            cp.start()

    def wait_a(m):
        wait_into(abuf.at[:, 0, mchunk(m), :], ab_r.at[m])

    a_load.wait()
    own_send(0)
    own_send(1)

    wait_into(away, x_r.at[0])
    s2_start(is_home, False, 0, 1)
    s2_start(is_home, True, 3)
    s2_start(is_away, False, 2, 3)

    def piece(n, e, x_, i):
        blk, row = place(x_, zl, (zh + e) % 2, i)
        return lbuf.at[n, blk, row]

    xm, xp, xo = (x + 3) % 4, (x + 1) % 4, (x + 2) % 4

    def s3(n, e, i):
        k = 2 * n + e
        return [rcopy(piece(n, e, x, i), piece(n, e, x, i), s_s.at[2], s3_r.at[k, 0], at_x(1)),
                rcopy(piece(n, e, x, i), piece(n, e, x, i), s_s.at[2], s3_r.at[k, 1], at_x(3))]

    def s3_relay(n, e):
        k = 2 * n + e
        return [rcopy(piece(n, e, xm, 0), piece(n, e, xm, 0), s_s.at[2], s3_r.at[k, 2], at_x(1)),
                rcopy(piece(n, e, xp, 1), piece(n, e, xp, 1), s_s.at[2], s3_r.at[k, 2], at_x(3))]

    def wait_pair(sem):
        wait_into(lbuf.at[0, pl.ds(0, 2), pl.ds(0, quart)], sem)

    def spread_x(n):
        for e in range(2):
            wait_pair(s2_r.at[2 * n + e])
            for i in range(2):
                for cp in s3(n, e, i):
                    cp.start()

    def relay_x(n):
        for e in range(2):
            cps = s3_relay(n, e)
            wait_pair(s3_r.at[2 * n + e, 0])
            cps[0].start()
            wait_pair(s3_r.at[2 * n + e, 1])
            cps[1].start()

    def wait_x(n):
        for e in range(2):
            wait_pair(s3_r.at[2 * n + e, 2])

    is_end = zl * (3 - zl) == 0
    def cout(m, n):
        return csend.at[n, pl.ds(first[m] + 16 * m, 16 + CHUNKS[m] * AB)]

    def c_copy(m, n, far=False):
        to, slot = (other[2], 3) if far else (other[n], n)
        t = pl.ds(0, 16 + CHUNKS[m] * AB)
        return rcopy(cout(m, n), crecv.at[m, slot, t], s_s.at[5], c_r.at[m, slot], at_z(zh * 4 + to))

    def code(part, dst, step=AB):
        n = part.shape[0]
        at = lax.broadcasted_iota(jnp.int32, (16, AB), 0)
        powers = jnp.zeros((16, AB), jnp.float32)
        for t in range(n // step):
            b = part[t * step:(t + 1) * step, :]
            top = jnp.max(jnp.abs(b), axis=0, keepdims=True)
            e = jnp.clip(jnp.floor(jnp.log2(jnp.maximum(top, 1e-30))) + 1.0, -90.0, 90.0)
            v = jnp.clip(jnp.round(b * jnp.exp2(15.0 - e)), -32767.0, 32767.0)
            dst[16 + t * step:16 + (t + 1) * step, :] = v.astype(jnp.int32).astype(jnp.int16)
            powers = jnp.where(at == t, e, powers)
        dst[0:16, :] = powers.astype(jnp.int32).astype(jnp.int16)

    def decode(src, t=0, step=AB):
        v = src[16 + t * step:16 + (t + 1) * step, :].astype(jnp.int32).astype(jnp.float32)
        e = src[0:16, :].astype(jnp.int32).astype(jnp.float32)
        return v * jnp.exp2(e[t:t + 1, :] - 15.0)

    is_inner = zl * (3 - zl) != 0

    def compute(m, n0, n1):
        r = mchunk(m)
        n = CHUNKS[m] * AB
        ln = pl.ds(n0 * AB, (n1 - n0) * AB)
        a = jnp.concatenate([abuf[yy, cc, r, :] for yy in range(4) for cc in range(2)], axis=1)
        b = jnp.concatenate([lbuf[j].reshape(8 * kw, AB) for j in range(n0, n1)], axis=1)
        acc[0:n, ln] = jnp.dot(a, b, preferred_element_type=jnp.float32)
        if n0 == 0:
            code(acc[0:n, AB:2 * AB], cout(m, 1))
            pl.when(is_end)(lambda: c_copy(m, 1, True).start())
            pl.when(is_inner)(lambda: c_copy(m, 1).start())
            ckeep[m, 0:n, :] = acc[0:n, 0:AB]

            @pl.when(is_end)
            def _():
                code(ckeep[m, 0:n, :], cout(m, 0))
                c_copy(m, 0).start()

        if n0 <= 2 < n1:
            code(acc[0:n, 2 * AB:3 * AB], cout(m, 2))
            c_copy(m, 2).start()
        if n1 == 4:
            cown[r, :] = acc[0:n, 3 * AB:4 * AB]

    def wait_c(m, slot):
        wait_into(crecv.at[m, slot, pl.ds(0, 16 + CHUNKS[m] * AB)], c_r.at[m, slot])

    def merge(m):
        @pl.when(is_inner)
        def _():
            wait_c(m, 3)
            for t in range(CHUNKS[m]):
                ckeep[m, t * AB:(t + 1) * AB, :] += decode(crecv.at[m, 3], t)
            code(ckeep[m, 0:CHUNKS[m] * AB, :], cout(m, 0))
            c_copy(m, 0).start()

    def add_slot(m, n):
        wait_c(m, n)
        for t in range(CHUNKS[m]):
            cown[first[m] + t * AB:first[m] + (t + 1) * AB, :] += decode(crecv.at[m, n], t)

    def out_copy(m):
        return pltpu.make_async_copy(out_v.at[:, mchunk(m)], out_ref.at[:, mchunk(m)], out_s.at[0])

    def value(m, t):
        at = first[m] + t * AB
        return -(cown[at:at + AB, :] * live[at // AB:at // AB + 1, :])

    def store_out(m):
        for t in range(CHUNKS[m]):
            at = first[m] + t * AB
            out_v[:, at:at + AB] = value(m, t).T.astype(jnp.bfloat16)
        out_copy(m).start()

    def finish_c(m):
        n = CHUNKS[m] * AB
        add_slot(m, 2)
        pl.when(is_inner)(lambda: add_slot(m, 1))
        add_slot(m, 0)
        for t in range(CHUNKS[m]):
            abf[t * AB:(t + 1) * AB, :] = value(m, t).astype(jnp.bfloat16)
        lhs = jnp.concatenate([lead[j, first[m] // half, pl.ds(first[m] % half, n), :] for j in range(4)], axis=1)
        part = lax.dot_general(lhs, abf[0:n, :], (((0,), (0,)), ((), ())), preferred_element_type=jnp.float32)
        corr[...] = part if m == 0 else corr[...] + part

    def wait_lead():
        h_loc.wait()
        wait_into(lead.at[pl.ds(0, 2)], h_r.at[1])

    def fwd_lead():
        wait_into(hblk(zmate, c), h_r.at[0])
        h_fwd.start()

    def sent():
        wait_into(away, s_s.at[0])
        wait_into(abuf.at[0, 0, pl.ds(0, 14 * quart * AB // kw), :], s_s.at[1])
        wait_into(abuf.at[0], s_s.at[2])
        wait_into(abuf.at[:, :, pl.ds(0, rows * 7 // 8), :], s_s.at[3])
        wait_into(lead.at[pl.ds(0, 3)], s_s.at[4])

    steps = {f.__name__: f for f in (
        spread_x, relay_x, wait_x, own_send, relay_a, finish_a, wait_a, send_lead, fwd_lead, wait_lead,
        compute, merge, sent, finish_c)}

    def run(plan):
        for name, *at in plan:
            steps[name](*at)

    run(FIRST)
    run(REST)
    pl.when(is_inner)(lambda: run(INNER))
    pl.when(is_end)(lambda: run(END))
    wait_into(csend, s_s.at[5])

    lrows = diag_ref.shape[0]

    def mine(p_):
        return pl.ds(pl.multiple_of(p_ * lrows, lrows), lrows)

    for d in (6, 5, 7, 4, 2, 1, 3):
        to = (zh + d // 4) % 2 * 4 + (x + d) % 4
        code(corr[mine(to), :], dsend.at[d - 1], lrows)
        cp = rcopy(dsend.at[d - 1], drecv.at[d - 1], s_s.at[6], x_r.at[1], (to, q))
        cp.start()
    for m in range(MCH):
        store_out(m)
    total = corr[mine(p), :]
    wait_into(drecv, x_r.at[1])
    for d in range(1, 8):
        total = total + decode(drecv.at[d - 1], 0, lrows)
    lead_id = p * lrows + lax.broadcasted_iota(jnp.int32, (lrows, AB), 0)
    keep = jnp.where(lead_id < sn_ref[k], 1.0, 0.0) * col_live
    piv_load.wait()
    diag_v[...] = (piv[...] - total) * keep
    diag_copy = pltpu.make_async_copy(diag_v, diag_ref, out_s.at[1])
    diag_copy.start()
    wait_into(dsend, s_s.at[6])
    pltpu.make_async_copy(out_v, out_ref, out_s.at[0]).wait()
    diag_copy.wait()


def per_device(ancestor_inverse, factor_panel, pivot_inverse, sn_size, anc_list):
    rows, cols = factor_panel.shape
    kw = ancestor_inverse.shape[1]
    lrows = pivot_inverse.shape[0]
    vm, dma = pltpu.VMEM, pltpu.SemaphoreType.DMA
    bf, f32 = jnp.bfloat16, jnp.float32
    anys = pl.BlockSpec(memory_space=pl.ANY)
    return pl.pallas_call(
        kernel,
        out_shape=(jax.ShapeDtypeStruct((cols, rows), bf),
                   jax.ShapeDtypeStruct((lrows, cols), f32)),
        in_specs=[anys, anys, anys, pl.BlockSpec(memory_space=pltpu.SMEM), anys],
        out_specs=(anys, anys),
        scratch_shapes=[
            vm((4, 2, rows, kw), bf),
            vm((rows, cols), bf),
            vm((lrows, cols), f32),
            vm(anc_list.shape, jnp.int32),
            vm((2, rows // 2, cols), bf),
            vm((2, 2, rows // 8, cols), bf),
            vm((4, 4, 2 * kw, cols), bf),
            vm((4, 2, rows // 2, cols), bf),
            vm((16, cols), f32),
            vm((TOP * AB, 4 * cols), f32),
            vm((rows, cols), f32),
            vm((3, rows + 16 * MCH, cols), jnp.int16),
            vm((MCH, 4, 16 + TOP * AB, cols), jnp.int16),
            vm((MCH, TOP * AB, cols), f32),
            vm((TOP * AB, cols), bf),
            vm((W, cols), f32),
            vm((7, lrows + 16, cols), jnp.int16),
            vm((7, lrows + 16, cols), jnp.int16),
            vm((cols, rows), bf),
            vm((lrows, cols), f32),
            dma((4,)), dma((7,)), dma((2,)), dma((8,)), dma((8, 3)),
            dma((MCH, 2)), dma((MCH,)), dma((MCH, 4)), dma((3,)), dma((2,)),
        ],
        compiler_params=pltpu.CompilerParams(
            collective_id=0, has_side_effects=True, vmem_limit_bytes=60 * 1024 * 1024),
        cost_estimate=pl.CostEstimate(flops=5_000_000_000, bytes_accessed=4_000_000, transcendentals=0),
    )(ancestor_inverse, factor_panel, pivot_inverse, sn_size, anc_list)


def solution(mesh):
    return jax.shard_map(
        per_device,
        mesh=mesh,
        in_specs=(P("prow", "pcol"), P("prow", "pcol"), P("prow", "pcol"), P(), P()),
        out_specs=(P("pcol", "prow"), P("prow", "pcol")),
        check_vma=False,
    )
```
